256 devices in a mesh: shard: 8 (over y_lo, x), lon: 32 (over z, y_hi, core).
Axes of the slice: x: 4, y: 4 (y_hi: 2, y_lo: 2; y = y_hi * 2 + y_lo), z: 8, core: 2. Of those that a mesh axis runs over, the one named last changes fastest.
Arguments:
- fields: bfloat16 [8, 48, 128, 1024], P('shard', None, 'lon'), may hold values from -6 to 6
- conv_kernel: float32 [3, 3, 1024], replicated, may hold values from -1.8 to 1.8
- gate_weight: bfloat16 [1024, 4096], P(None, 'shard'), may hold values from -0.1875 to 0.1875
- up_weight: bfloat16 [1024, 4096], P(None, 'shard'), may hold values from -0.1875 to 0.1875
- down_weight: bfloat16 [4096, 1024], P('shard'), may hold values from -0.09375 to 0.09375
- cotangent: bfloat16 [8, 48, 128, 1024], P('shard', None, 'lon'), may hold values from -6 to 6
Outputs:
- mlp_out: bfloat16 [8, 48, 128, 1024], P('shard', None, 'lon')
- input_grad: bfloat16 [8, 48, 128, 1024], P('shard', None, 'lon')
- grad_gate: float32 [1024, 4096], P('lon', 'shard')
- grad_up: float32 [1024, 4096], P('lon', 'shard')
- grad_down: float32 [4096, 1024], P('shard', 'lon')
- grad_kernel: float32 [3, 3, 1024], replicated
The draws below stay inside these ranges and needn't reach their ends.
All inputs are finite; a program needn't handle non-finite values.
Results may differ from the reference program's by a relative error of at most 0.02.
Values may be sent and summed in bfloat16 or wider, within the bound.
A program may use at most 128 MiB of HBM per device.

```python
import jax
import jax.numpy as jnp
from jax import lax

D = 1024
FF = 4096
LAT = 48
SAMPLES = 8
LON = 128
TOKENS = 49152
N_SHARD = 8


def level_of(rng, extent, pieces, smallest, high):
    gain = 1.0
    for position, blocks in pieces:
        steps = jax.random.uniform(jax.random.fold_in(jax.random.fold_in(rng, 6), position), (blocks,), jnp.float32, smallest / len(pieces), high / len(pieces))
        gain = gain * jnp.repeat(jnp.exp(steps), extent[position] // blocks).reshape((-1,) + (1,) * (len(extent) - 1 - position))
    return gain


def centred(rng, dims, scale, limit, pieces=(), kind=jnp.bfloat16):
    gain = level_of(rng, dims, pieces, -0.22, 0.18) if pieces else 1.0
    entries = jax.random.normal(rng, dims, jnp.float32) * scale * gain
    return jnp.minimum(jnp.maximum(entries, -limit), limit).astype(kind)


def setup_inputs(seed: int = 0) -> dict:
    streams_of = jax.random.split(jax.random.key(seed), 7)
    fields = centred(streams_of[0], (SAMPLES, LAT, LON, D), 1.0, 6.0, ((0, 8), (2, 32)))
    conv_kernel = centred(streams_of[1], (3, 3, D), 0.3, 1.8, (), jnp.float32)
    gate_weight = centred(streams_of[2], (D, FF), D ** -0.5, 0.1875, ((1, 8),))
    up_weight = centred(streams_of[3], (D, FF), D ** -0.5, 0.1875, ((1, 8),))
    down_weight = centred(streams_of[4], (FF, D), FF ** -0.5, 0.09375, ((0, 8),))
    cotangent = centred(streams_of[5], (SAMPLES, LAT, LON, D), 1.0, 6.0, ((0, 8), (2, 32)))
    return {"fields": fields, "conv_kernel": conv_kernel, "gate_weight": gate_weight, "up_weight": up_weight, "down_weight": down_weight, "cotangent": cotangent}


def stencil(widened, kernel):
    height = widened.shape[-3]
    breadth = widened.shape[-2] - 2
    pad_config = [(0, 0)] * (widened.ndim - 3) + [(1, 1), (0, 0), (0, 0)]
    padded = jnp.pad(widened, pad_config)
    summed = jnp.zeros(widened.shape[:-3] + (height, breadth, widened.shape[-1]), jnp.float32)
    for lat_off in range(3):
        for lon_off in range(3):
            summed = summed + kernel[lat_off, lon_off] * padded[..., lat_off:lat_off + height, lon_off:lon_off + breadth, :]
    return summed


def kernel_terms(grad_field, widened):
    height = widened.shape[-3]
    breadth = widened.shape[-2] - 2
    pad_config = [(0, 0)] * (widened.ndim - 3) + [(1, 1), (0, 0), (0, 0)]
    padded = jnp.pad(widened, pad_config)
    lead_axes = tuple(range(grad_field.ndim - 1))
    listed = []
    for lat_off in range(3):
        for lon_off in range(3):
            window = padded[..., lat_off:lat_off + height, lon_off:lon_off + breadth, :]
            listed.append(jnp.sum(grad_field * window, axis=lead_axes))
    return jnp.stack(listed).reshape(3, 3, grad_field.shape[-1])


def wrap_columns(field):
    return jnp.concatenate([field[:, -1:], field, field[:, :1]], axis=1)


def block_sum(parts):
    rounded = lax.optimization_barrier(parts.astype(jnp.bfloat16))
    return jnp.sum(rounded.astype(jnp.float32), axis=0)


def reference(fields, conv_kernel, gate_weight, up_weight, down_weight, cotangent):
    grad_scale = 1.0 / (float(TOKENS) ** 0.5)
    block_width = FF // N_SHARD
    flipped = conv_kernel[::-1, ::-1]
    gate_blocks = gate_weight.reshape(D, N_SHARD, block_width).astype(jnp.float32)
    up_blocks = up_weight.reshape(D, N_SHARD, block_width).astype(jnp.float32)
    down_blocks = down_weight.reshape(N_SHARD, block_width, D).astype(jnp.float32)
    highest = lax.Precision.HIGHEST

    def per_sample(carry, inputs):
        sample, tangent = inputs
        sample_f = sample.astype(jnp.float32)
        widened = wrap_columns(sample_f)
        mixed = (sample_f + stencil(widened, conv_kernel)).astype(jnp.bfloat16)
        flat_mixed = mixed.reshape(-1, D)
        gate = jnp.dot(flat_mixed, gate_weight, preferred_element_type=jnp.float32)
        up_value = jnp.dot(flat_mixed, up_weight, preferred_element_type=jnp.float32)
        sigmas = jax.nn.sigmoid(gate)
        hidden = (gate * sigmas * up_value).astype(jnp.bfloat16)
        hidden_blocks = hidden.reshape(-1, N_SHARD, block_width).astype(jnp.float32)
        out_parts = jnp.einsum("rnf,nfd->nrd", hidden_blocks, down_blocks, precision=highest)
        output = block_sum(out_parts).astype(jnp.bfloat16).reshape(LAT, LON, D)
        flat_tangent = tangent.reshape(-1, D)
        dhidden = jnp.dot(flat_tangent, down_weight.T, preferred_element_type=jnp.float32)
        dgate = (dhidden * up_value * sigmas * (1.0 + gate * (1.0 - sigmas))).astype(jnp.bfloat16)
        dup = (dhidden * gate * sigmas).astype(jnp.bfloat16)
        back_parts = jnp.einsum("rnf,dnf->nrd", dgate.reshape(-1, N_SHARD, block_width).astype(jnp.float32), gate_blocks, precision=highest)
        back_parts = back_parts + jnp.einsum("rnf,dnf->nrd", dup.reshape(-1, N_SHARD, block_width).astype(jnp.float32), up_blocks, precision=highest)
        dmixed = block_sum(back_parts).astype(jnp.bfloat16).astype(jnp.float32).reshape(LAT, LON, D)
        in_grad = (dmixed + stencil(wrap_columns(dmixed), flipped)).astype(jnp.bfloat16)
        kernel_part = kernel_terms(dmixed, widened)
        gate_acc, up_acc, down_acc, kernel_acc = carry
        gate_acc = gate_acc + jnp.dot(flat_mixed.T, dgate, preferred_element_type=jnp.float32)
        up_acc = up_acc + jnp.dot(flat_mixed.T, dup, preferred_element_type=jnp.float32)
        down_acc = down_acc + jnp.dot(hidden.T, flat_tangent, preferred_element_type=jnp.float32)
        kernel_acc = kernel_acc + kernel_part
        return (gate_acc, up_acc, down_acc, kernel_acc), (output, in_grad)

    init = (jnp.zeros((D, FF), jnp.float32), jnp.zeros((D, FF), jnp.float32), jnp.zeros((FF, D), jnp.float32), jnp.zeros((3, 3, D), jnp.float32))
    totals, results = lax.scan(per_sample, init, (fields, cotangent))
    mlp_out, input_grad = results
    return mlp_out, input_grad, totals[0] * grad_scale, totals[1] * grad_scale, totals[2] * grad_scale, totals[3] * grad_scale
```

```python
import jax
import jax.numpy as jnp
from jax import lax
from jax.experimental import pallas as pl
from jax.experimental.pallas import tpu as pltpu
from jax.sharding import PartitionSpec as P

MESH = pl.DeviceIdType.MESH
F32, BF16 = jnp.float32, jnp.bfloat16
NX, NY, NZ, NC = 4, 4, 8, 2
NN = (((1,), (0,)), ((), ()))
NT = (((1,), (1,)), ((), ()))
N_SEM = 128


def mm(a, b, dims=NN):
    return lax.dot_general(a, b, dims, preferred_element_type=F32)


def kernel(
    grad_scale, f_ref, k_ref, wg, wu, wd, t_ref,
    o_out, o_in, o_gg, o_gu, o_gd, o_gk,
    halo, dhalo, wg2, wu2, wd2, mix, cot, hid, dg, du, pb, po, rb3, rb1, ro3, ro1,
    mix_t, cot_t, gb, rc, ry, gz, rz, dm, kp, rk1, rk2, rk3, kf, ssem, rsem,
):
    width, lat = f_ref.shape[2], f_ref.shape[1]
    tok = 4 * lat
    half = tok // 2
    ff = wg.shape[1]
    s, l = lax.axis_index("shard"), lax.axis_index("lon")
    x, yl = lax.rem(s, 4), s // 4
    z, yh, c = l // 4, lax.rem(l // 2, 2), lax.rem(l, 2)
    y = yh * 2 + yl

    def dev(dx=0, dy=0, dz=0, dc=0):
        x2 = lax.rem(x + dx + NX, NX)
        y2 = lax.rem(y + dy + NY, NY)
        z2 = lax.rem(z + dz + NZ, NZ)
        c2 = lax.rem(c + dc, NC)
        return (lax.rem(y2, 2) * 4 + x2, z2 * 4 + (y2 // 2) * 2 + c2)

    lon_up = (s, lax.rem(l + 1, 32))
    lon_down = (s, lax.rem(l + 31, 32))
    squad = [(dx, dc) for dx in range(NX) for dc in range(NC) if (dx, dc) != (0, 0)]
    partners = [dev(dx=dx, dc=dc) for dx, dc in squad]
    partners += [dev(dy=d) for d in range(1, NY)]
    partners += [dev(dz=d) for d in range(1, NZ)]
    partners += [lon_up, lon_down]

    barrier = pltpu.get_barrier_semaphore()
    for p in partners:
        pl.semaphore_signal(barrier, inc=1, device_id=p, device_id_type=MESH)
    pl.semaphore_wait(barrier, len(partners))

    started = []

    def send(src, dst, to):
        i = len(started)
        copy = pltpu.make_async_remote_copy(
            src_ref=src, dst_ref=dst, send_sem=ssem.at[i], recv_sem=rsem.at[i],
            device_id=to, device_id_type=MESH,
        )
        copy.start()
        started.append(copy)
        return copy

    def rows(ref, r0, n):
        return ref.at[pl.ds(r0, n)]

    c_halo = [send(f_ref.at[3], halo.at[0], lon_up), send(f_ref.at[0], halo.at[1], lon_down)]
    slot1, slot2, slot3 = tok, 2 * tok, 3 * tok
    c_cot = [
        send(t_ref, rows(cot, slot1, tok), dev(dx=1)),
        send(t_ref, rows(cot, slot2, tok), dev(dx=-1)),
    ]
    c_w = []
    for own, other in ((wd, wd2), (wg, wg2), (wu, wu2)):
        n = own.shape[0] // 4
        q_up, q_down = rows(own, c * n, n), rows(own, (2 + c) * n, n)
        c_w.append((
            send(q_up, rows(other, c * n, n), dev(dy=1)),
            send(q_down, rows(other, (2 + c) * n, n), dev(dy=-1)),
            other, n,
        ))
    cot[pl.ds(0, tok), :] = t_ref[...]

    row = lax.broadcasted_iota(jnp.int32, (lat, 128), 0)

    def down(v):
        return jnp.where(row == 0, 0.0, pltpu.roll(v, 1, 0))

    def up(v):
        return jnp.where(row == lat - 1, 0.0, pltpu.roll(v, lat - 1, 0))

    def conv(src, edges, flip, store):
        def tile(t, carry):
            cs = pl.ds(pl.multiple_of(t * 128, 128), 128)
            cols = [edges[0, :, cs]] + [src[j, :, cs] for j in range(4)] + [edges[1, :, cs]]
            cols = [v.astype(F32) for v in cols]
            taps = [k_ref[8 - i if flip else i, cs].reshape(1, 128) for i in range(9)]
            for j in range(4):
                a0, a1, a2 = (
                    sum(taps[3 * a + b] * cols[j + b] for b in range(3)) for a in range(3)
                )
                store(j, cs, (cols[j + 1] + a1 + down(a0) + up(a2)).astype(BF16))
            return carry

        lax.fori_loop(0, width // 128, tile, 0)

    for cp in c_halo:
        cp.wait_recv()

    def store_mixed(j, cs, v):
        mix[pl.ds(j * lat, lat), cs] = v

    conv(f_ref, halo, False, store_mixed)
    c_mix = [
        send(rows(mix, 0, tok), rows(mix, slot1, tok), dev(dx=1)),
        send(rows(mix, 0, tok), rows(mix, slot2, tok), dev(dx=-1)),
    ]

    weights = ((wg, wu, wd), (wg2, wu2, wd2))

    def proc(r0, n, h):
        wgr, wur, wdr = weights[h]

        def tile(t, carry):
            cs = pl.ds(pl.multiple_of(t * 256, 256), 256)
            m = mix[pl.ds(r0, n), :]
            gate = mm(m, wgr[:, cs])
            value = mm(m, wur[:, cs])
            dhid = mm(cot[pl.ds(r0, n), :], wdr[cs, :], NT)
            sig = 1.0 / (1.0 + jnp.exp(-gate))
            act = gate * sig
            oc = pl.ds(pl.multiple_of(h * ff + t * 256, 256), 256)
            hid[pl.ds(r0, n), oc] = (act * value).astype(BF16)
            dg[pl.ds(r0, n), oc] = (dhid * value * sig * (1.0 + gate * (1.0 - sig))).astype(BF16)
            du[pl.ds(r0, n), oc] = (dhid * act).astype(BF16)
            return carry

        lax.fori_loop(0, ff // 256, tile, 0)

    def back(r0, n):
        def tile(t, carry):
            cs = pl.ds(pl.multiple_of(t * 256, 256), 256)
            acc = None
            for h in range(2):
                wgr, wur, _ = weights[h]
                hs = pl.ds(h * ff, ff)
                a = mm(dg[pl.ds(r0, n), hs], wgr[cs, :], NT)
                a = a + mm(du[pl.ds(r0, n), hs], wur[cs, :], NT)
                acc = a if acc is None else acc + a
            pb[pl.ds(r0, n), cs] = acc.astype(BF16)
            return carry

        lax.fori_loop(0, width // 256, tile, 0)

    def outp(r0, n):
        def tile(t, carry):
            cs = pl.ds(pl.multiple_of(t * 256, 256), 256)
            acc = mm(hid[pl.ds(r0, n), pl.ds(0, ff)], wd[:, cs])
            acc = acc + mm(hid[pl.ds(r0, n), pl.ds(ff, ff)], wd2[:, cs])
            po[pl.ds(r0, n), cs] = acc.astype(BF16)
            return carry

        lax.fori_loop(0, width // 256, tile, 0)

    def forward(copies, buf):
        copies[0].wait_recv()
        a = send(rows(buf, slot1, half), rows(buf, slot3, half), dev(dx=1))
        copies[1].wait_recv()
        b = send(rows(buf, slot2 + half, half), rows(buf, slot3 + half, half), dev(dx=-1))
        return [a, b]

    def share(i):
        cu, cd, other, n = c_w[i]
        cu.wait_recv()
        cd.wait_recv()
        return [
            send(rows(other, c * n, n), rows(other, c * n, n), dev(dc=1)),
            send(rows(other, (2 + c) * n, n), rows(other, (2 + c) * n, n), dev(dc=1)),
        ]

    proc(0, tok, 0)
    f_cot = forward(c_cot, cot)
    c_share = share(0)
    c_share += share(1)
    f_mix = forward(c_mix, mix)
    proc(tok, 2 * tok, 0)
    c_share += share(2)
    for cp in c_share:
        cp.wait_recv()
    proc(0, 3 * tok, 1)
    for cp in f_cot + f_mix:
        cp.wait_recv()
    proc(slot3, tok, 0)
    proc(slot3, tok, 1)

    def spread3(part, far):
        return [
            send(rows(part, slot3, half), far.at[0], dev(dx=-1)),
            send(rows(part, slot3 + half, half), far.at[1], dev(dx=1)),
        ]

    def spread1(part, near):
        return [
            send(rows(part, slot1 + half, half), near.at[0, pl.ds(half, half)], dev(dx=-1)),
            send(rows(part, slot2, half), near.at[1, pl.ds(0, half)], dev(dx=1)),
        ]

    def merge(part, far, copies, near):
        copies[0].wait_recv()
        r = pl.ds(slot1, half)
        part[r, :] = (part[r, :].astype(F32) + far[0].astype(F32)).astype(BF16)
        a = send(rows(part, slot1, half), near.at[0, pl.ds(0, half)], dev(dx=-1))
        copies[1].wait_recv()
        r = pl.ds(slot2 + half, half)
        part[r, :] = (part[r, :].astype(F32) + far[1].astype(F32)).astype(BF16)
        b = send(rows(part, slot2 + half, half), near.at[1, pl.ds(half, half)], dev(dx=1))
        return [a, b]

    back(slot3, tok)
    c_b3 = spread3(pb, rb3)
    back(tok, 2 * tok)
    c_b1 = spread1(pb, rb1)
    outp(slot3, tok)
    c_o3 = spread3(po, ro3)
    outp(tok, 2 * tok)
    c_o1 = spread1(po, ro1)

    def transpose(src, dst):
        for pair in range(2):
            for b in range(width // 128):
                v = src[pl.ds(pair * 2 * tok, 2 * tok), pl.ds(b * 128, 128)].T
                for q in range(4):
                    dst[q % 2, q // 2, pl.ds(b * 32, 32), pl.ds(pair * 2 * tok, 2 * tok)] = v[
                        q * 32 : q * 32 + 32
                    ]

    def weight_grad(g, lhs, rhs):
        for cc in (1 - c, c):
            for h in range(2):
                yl2 = yl if h == 0 else 1 - yl

                def tile(t, carry, cc=cc, h=h, yl2=yl2):
                    yh2, n2 = t // 2, lax.rem(t, 2)
                    cs = pl.ds(pl.multiple_of(h * ff + n2 * 256, 256), 256)
                    v = mm(lhs[cc, yh2], rhs[:, cs]) * grad_scale
                    gb[g, cc, yh2 * 2 + yl2, :, pl.ds(pl.multiple_of(n2 * 256, 256), 256)] = (
                        v.astype(BF16)
                    )
                    return carry

                lax.fori_loop(0, 4, tile, 0)
            if cc is not c:
                cp = send(gb.at[g, cc], rc.at[g], dev(dc=1))
        return cp

    def add_core(g, cp):
        cp.wait_recv()

        def tile(t, carry):
            gb[g, c, t] = (gb[g, c, t].astype(F32) + rc[g, t].astype(F32)).astype(BF16)
            return carry

        lax.fori_loop(0, NY, tile, 0)
        return [send(gb.at[g, c, lax.rem(y + d, NY)], ry.at[g, d - 1], dev(dy=d)) for d in (1, 3, 2)]

    def add_y(g, cps):
        for cp in cps:
            cp.wait_recv()
        v = gb[g, c, y].astype(F32)
        for d in range(NY - 1):
            v = v + ry[g, d].astype(F32)
        gz[g] = v.astype(BF16).reshape(NZ, 32, ff)
        return [
            send(gz.at[g, lax.rem(z + d, NZ)], rz.at[g, d - 1], dev(dz=d))
            for d in (4, 3, 5, 2, 6, 1, 7)
        ]

    def add_z(g, cps, out):
        for cp in cps:
            cp.wait_recv()
        v = gz[g, z].astype(F32)
        for d in range(NZ - 1):
            v = v + rz[g, d].astype(F32)
        out[...] = v

    transpose(mix, mix_t)
    g0 = weight_grad(0, mix_t, dg)
    c_b1 += merge(pb, rb3, c_b3, rb1)
    g1 = weight_grad(1, mix_t, du)
    y0 = add_core(0, g0)
    c_o1 += merge(po, ro3, c_o3, ro1)
    transpose(cot, cot_t)
    g2 = weight_grad(2, cot_t, hid)
    y1 = add_core(1, g1)
    back(0, tok)
    outp(0, tok)
    y2 = add_core(2, g2)

    def total(part, near, copies, store):
        for cp in copies:
            cp.wait_recv()
        for j in range(4):
            r = pl.ds(j * lat, lat)
            v = part[r, :].astype(F32) + near[0, r, :].astype(F32) + near[1, r, :].astype(F32)
            store(j, v.astype(BF16))

    def store_dm(j, v):
        dm[j] = v

    total(pb, rb1, c_b1, store_dm)
    c_dh = [send(dm.at[3], dhalo.at[0], lon_up), send(dm.at[0], dhalo.at[1], lon_down)]

    def kernel_tile(e, carry):
        cs = pl.ds(pl.multiple_of(e * 128, 128), 128)
        cols = [halo[0, :, cs]] + [f_ref[j, :, cs] for j in range(4)] + [halo[1, :, cs]]
        cols = [v.astype(F32) for v in cols]
        sums = [None] * 9
        for j in range(4):
            d = dm[j, :, cs].astype(F32)
            for a, v in enumerate((up(d), d, down(d))):
                for b in range(3):
                    p = v * cols[j + b]
                    i = 3 * a + b
                    sums[i] = p if sums[i] is None else sums[i] + p
        for i in range(9):
            kp[e, pl.ds(i, 1), :] = jnp.sum(sums[i], axis=0, keepdims=True) * grad_scale
        return carry

    kp[...] = jnp.zeros(kp.shape, F32)
    lax.fori_loop(0, NX * NC, kernel_tile, 0)
    me = 2 * x + c
    c_k = []
    for i, (dx, dc) in enumerate(squad):
        to = 2 * lax.rem(x + dx, NX) + lax.rem(c + dc, NC)
        c_k.append(send(kp.at[to], rk1.at[i], dev(dx=dx, dc=dc)))

    z0 = add_y(0, y0)

    for cp in c_k:
        cp.wait_recv()
    v = kp[me]
    for i in range(len(squad)):
        v = v + rk1[i]
    rk2[y] = v
    c_k = [send(rk2.at[y], rk2.at[y], dev(dy=d)) for d in range(1, NY)]

    for cp in c_dh:
        cp.wait_recv()

    def store_in(j, cs, v):
        o_in[j, :, cs] = v

    conv(dm, dhalo, True, store_in)

    for cp in c_k:
        cp.wait_recv()
    rk3[z] = rk2[0] + rk2[1] + rk2[2] + rk2[3]
    c_k = [send(rk3.at[z], rk3.at[z], dev(dz=d)) for d in range(1, NZ)]

    z1 = add_y(1, y1)

    for cp in c_k:
        cp.wait_recv()
    v = rk3[0]
    for i in range(1, NZ):
        v = v + rk3[i]
    kf[me] = v
    c_k = [send(kf.at[me], kf.at[me], dev(dx=dx, dc=dc)) for dx, dc in squad]

    def store_out(j, v):
        o_out[pl.ds(j * lat, lat), :] = v

    total(po, ro1, c_o1, store_out)
    z2 = add_y(2, y2)
    add_z(0, z0, o_gg)
    add_z(1, z1, o_gu)
    for cp in c_k:
        cp.wait_recv()
    for e in range(NX * NC):
        o_gk[:, pl.ds(e * 128, 128)] = kf[e]
    add_z(2, z2, o_gd)
    for cp in started:
        cp.wait_send()


def shards(fields, conv_kernel, gate_weight, up_weight, down_weight, cotangent):
    _, lat, lon, width = fields.shape
    ff = gate_weight.shape[1]
    tok = lat * lon
    total_tokens = tok * lax.axis_size("shard") * lax.axis_size("lon")
    grad_scale = 1.0 / float(total_tokens) ** 0.5
    field_cols = fields[0].transpose(1, 0, 2)
    tangent = cotangent[0].transpose(1, 0, 2).reshape(tok, width)
    taps = conv_kernel.reshape(9, width)
    rows_d = width // 32
    vmem = lambda *shape, dtype=BF16: pltpu.VMEM(shape, dtype)
    call = pl.pallas_call(
        lambda *refs: kernel(grad_scale, *refs),
        name="swiglu_block",
        out_shape=[
            jax.ShapeDtypeStruct((tok, width), BF16),
            jax.ShapeDtypeStruct((lon, lat, width), BF16),
            jax.ShapeDtypeStruct((rows_d, ff), F32),
            jax.ShapeDtypeStruct((rows_d, ff), F32),
            jax.ShapeDtypeStruct((rows_d, ff), F32),
            jax.ShapeDtypeStruct((16, width), F32),
        ],
        in_specs=[pl.BlockSpec(memory_space=pltpu.VMEM)] * 6,
        out_specs=[pl.BlockSpec(memory_space=pltpu.VMEM)] * 6,
        scratch_shapes=[
            vmem(2, lat, width),
            vmem(2, lat, width),
            vmem(width, ff),
            vmem(width, ff),
            vmem(ff, width),
            vmem(4 * tok, width),
            vmem(4 * tok, width),
            vmem(4 * tok, 2 * ff),
            vmem(4 * tok, 2 * ff),
            vmem(4 * tok, 2 * ff),
            vmem(4 * tok, width),
            vmem(4 * tok, width),
            vmem(2, tok // 2, width),
            vmem(2, tok, width),
            vmem(2, tok // 2, width),
            vmem(2, tok, width),
            vmem(2, 2, width // 4, 4 * tok),
            vmem(2, 2, width // 4, 4 * tok),
            vmem(3, 2, NY, width // 4, ff),
            vmem(3, NY, width // 4, ff),
            vmem(3, NY - 1, width // 4, ff),
            vmem(3, NZ, 32, ff),
            vmem(3, NZ - 1, 32, ff),
            vmem(lon, lat, width),
            vmem(8, 16, width // 8, dtype=F32),
            vmem(7, 16, width // 8, dtype=F32),
            vmem(NY, 16, width // 8, dtype=F32),
            vmem(NZ, 16, width // 8, dtype=F32),
            vmem(8, 16, width // 8, dtype=F32),
            pltpu.SemaphoreType.DMA((N_SEM,)),
            pltpu.SemaphoreType.DMA((N_SEM,)),
        ],
        compiler_params=pltpu.CompilerParams(
            collective_id=0, has_side_effects=True, vmem_limit_bytes=60 * 2**20
        ),
        cost_estimate=pl.CostEstimate(flops=14_500_000_000, bytes_accessed=6_000_000, transcendentals=800_000),
    )
    out, in_grad, gg, gu, gd, gk = call(
        field_cols, taps, gate_weight, up_weight, down_weight, tangent
    )

    def placed(v):
        return v.reshape(lon, lat, width).transpose(1, 0, 2)[None]

    return placed(out), placed(in_grad), gg, gu, gd.T, gk[:9].reshape(3, 3, width)


def solution(mesh):
    placed = (
        P("shard", None, "lon", None),
        P(),
        P(None, "shard"),
        P(None, "shard"),
        P("shard", None),
        P("shard", None, "lon", None),
    )
    return jax.shard_map(
        shards,
        mesh=mesh,
        in_specs=placed,
        out_specs=(
            P("shard", None, "lon", None),
            P("shard", None, "lon", None),
            P("lon", "shard"),
            P("lon", "shard"),
            P("shard", "lon"),
            P(),
        ),
        check_vma=False,
    )
```

```python
import jax
import jax.numpy as jnp
from jax import lax
from jax.experimental import pallas as pl
from jax.experimental.pallas import tpu as pltpu
from jax.sharding import PartitionSpec as P

MESH = pl.DeviceIdType.MESH
F32, BF16 = jnp.float32, jnp.bfloat16
NX, NY, NZ, NC = 4, 4, 8, 2
NN = (((1,), (0,)), ((), ()))
NT = (((1,), (1,)), ((), ()))
N_SEM = 128


def mm(a, b, dims=NN):
    return lax.dot_general(a, b, dims, preferred_element_type=F32)


def kernel(
    grad_scale, f_in, k_ref, wg_in, wu_in, wd_in, t_in,
    o_out, o_in, o_gg, o_gu, o_gd, o_gk,
    f_raw, t_raw, f_ref, wg, wu, wd, halo, dhalo, wg2, wu2, wd2, mix, cot, hid, dg, du, pb, po, rb3, rb1, ro3, ro1,
    dh, mix_t, cot_t, gb, rc, ry2, ry1, gz, rz, zr, gy, rzy, dm, kp, rk1, rk2, rk3, kf, ssem, rsem, lsem,
):
    width, lat = f_ref.shape[2], f_ref.shape[1]
    local = [
        pltpu.make_async_copy(src, dst, lsem.at[i])
        for i, (src, dst) in enumerate((
            (f_in, f_raw), (t_in, t_raw), (wd_in, wd), (wg_in, wg), (wu_in, wu),
        ))
    ]
    for cp in local:
        cp.start()
    tok = 4 * lat
    half = tok // 2
    ff = wg.shape[1]
    s, l = lax.axis_index("shard"), lax.axis_index("lon")
    x, yl = lax.rem(s, 4), s // 4
    z, yh, c = l // 4, lax.rem(l // 2, 2), lax.rem(l, 2)
    y = yh * 2 + yl

    def dev(dx=0, dy=0, dz=0, dc=0):
        x2 = lax.rem(x + dx + NX, NX)
        y2 = lax.rem(y + dy + NY, NY)
        z2 = lax.rem(z + dz + NZ, NZ)
        c2 = lax.rem(c + dc, NC)
        return (lax.rem(y2, 2) * 4 + x2, z2 * 4 + (y2 // 2) * 2 + c2)

    lon_up = (s, lax.rem(l + 1, 32))
    lon_down = (s, lax.rem(l + 31, 32))
    squad = [(dx, dc) for dx in range(NX) for dc in range(NC) if (dx, dc) != (0, 0)]
    partners = [dev(dx=dx, dc=dc) for dx, dc in squad]
    partners += [dev(dy=d) for d in range(1, NY)]
    partners += [dev(dz=d) for d in range(1, NZ)]
    partners += [lon_up, lon_down]

    barrier = pltpu.get_barrier_semaphore()
    for p in partners:
        pl.semaphore_signal(barrier, inc=1, device_id=p, device_id_type=MESH)
    pl.semaphore_wait(barrier, len(partners))

    started = []

    def send(src, dst, to):
        i = len(started)
        copy = pltpu.make_async_remote_copy(
            src_ref=src, dst_ref=dst, send_sem=ssem.at[i], recv_sem=rsem.at[i],
            device_id=to, device_id_type=MESH,
        )
        copy.start()
        started.append(copy)
        return copy

    def rows(ref, r0, n):
        return ref.at[pl.ds(r0, n)]

    local[0].wait()
    f_ref[...] = jnp.swapaxes(f_raw[...], 0, 1)
    c_halo = [send(f_ref.at[3], halo.at[0], lon_up), send(f_ref.at[0], halo.at[1], lon_down)]
    slot1, slot2, slot3 = tok, 2 * tok, 3 * tok
    local[1].wait()
    cot[pl.ds(0, tok), :] = jnp.swapaxes(t_raw[...], 0, 1).reshape(tok, width)
    c_cot = [
        send(rows(cot, 0, tok), rows(cot, slot1, tok), dev(dx=1)),
        send(rows(cot, 0, tok), rows(cot, slot2, tok), dev(dx=-1)),
    ]
    c_w = []
    for i, (own, other) in enumerate(((wd, wd2), (wg, wg2), (wu, wu2))):
        local[2 + i].wait()
        n = own.shape[0] // 4
        q_up, q_down = rows(own, c * n, n), rows(own, (2 + c) * n, n)
        c_w.append((
            send(q_up, rows(other, c * n, n), dev(dy=1)),
            send(q_down, rows(other, (2 + c) * n, n), dev(dy=-1)),
            other, n,
        ))

    row = lax.broadcasted_iota(jnp.int32, (lat, 128), 0)

    def down(v):
        return jnp.where(row == 0, 0.0, pltpu.roll(v, 1, 0))

    def up(v):
        return jnp.where(row == lat - 1, 0.0, pltpu.roll(v, lat - 1, 0))

    def conv(src, edges, flip, store):
        for t in range(width // 128):
            cs = pl.ds(t * 128, 128)
            cols = [edges[0, :, cs]] + [src[j, :, cs] for j in range(4)] + [edges[1, :, cs]]
            cols = [v.astype(F32) for v in cols]
            taps = [
                k_ref[2 - a if flip else a, 2 - b if flip else b, cs].reshape(1, 128)
                for a in range(3) for b in range(3)
            ]
            for j in range(4):
                a0, a1, a2 = (
                    sum(taps[3 * a + b] * cols[j + b] for b in range(3)) for a in range(3)
                )
                store(j, cs, (cols[j + 1] + a1 + down(a0) + up(a2)).astype(BF16))

    for cp in c_halo:
        cp.wait_recv()

    def store_mixed(j, cs, v):
        mix[pl.ds(j * lat, lat), cs] = v

    conv(f_ref, halo, False, store_mixed)
    c_mix = [
        send(rows(mix, 0, tok), rows(mix, slot1, tok), dev(dx=1)),
        send(rows(mix, 0, tok), rows(mix, slot2, tok), dev(dx=-1)),
    ]

    def transpose(src, dst, pair):
        r = pl.ds(pair * 2 * tok, 2 * tok)
        for b in range(width // 128):
            v = src[r, pl.ds(b * 128, 128)].T
            for q in range(4):
                dst[q % 2, pl.ds(q // 2 * 256 + b * 32, 32), r] = v[q * 32 : q * 32 + 32]

    weights = ((wg, wu, wd), (wg2, wu2, wd2))

    def proc_d(r0, n, h):
        wdr = weights[h][2]
        dh[pl.ds(r0, n), pl.ds(h * ff, ff)] = mm(cot[pl.ds(r0, n), :], wdr[...], NT)

    def proc_g(r0, n, h):
        wgr, wur, _ = weights[h]
        r = pl.ds(r0, n)
        for t in range(ff // 256):
            cs = pl.ds(t * 256, 256)
            oc = pl.ds(h * ff + t * 256, 256)
            gate = mm(mix[r, :], wgr[:, cs])
            value = mm(mix[r, :], wur[:, cs])
            dhid = dh[r, oc]
            sig = 1.0 / (1.0 + jnp.exp(-gate))
            act = gate * sig
            hid[r, oc] = (act * value).astype(BF16)
            dg[r, oc] = (dhid * value * sig * (1.0 + gate * (1.0 - sig))).astype(BF16)
            du[r, oc] = (dhid * act).astype(BF16)

    def back(r0, n):
        r = pl.ds(r0, n)
        for t in range(width // 512):
            cs = pl.ds(t * 512, 512)
            acc = None
            for h in range(2):
                wgr, wur, _ = weights[h]
                hs = pl.ds(h * ff, ff)
                a = mm(dg[r, hs], wgr[cs, :], NT) + mm(du[r, hs], wur[cs, :], NT)
                acc = a if acc is None else acc + a
            pb[r, cs] = acc.astype(BF16)

    def outp(r0, n):
        r = pl.ds(r0, n)
        for t in range(width // 512):
            cs = pl.ds(t * 512, 512)
            acc = mm(hid[r, pl.ds(0, ff)], wd[:, cs]) + mm(hid[r, pl.ds(ff, ff)], wd2[:, cs])
            po[r, cs] = acc.astype(BF16)

    def forward(copies, buf):
        copies[0].wait_recv()
        a = send(rows(buf, slot1, half), rows(buf, slot3, half), dev(dx=1))
        copies[1].wait_recv()
        b = send(rows(buf, slot2 + half, half), rows(buf, slot3 + half, half), dev(dx=-1))
        return [a, b]

    def share(i):
        cu, cd, other, n = c_w[i]
        cu.wait_recv()
        cd.wait_recv()
        return [
            send(rows(other, c * n, n), rows(other, c * n, n), dev(dc=1)),
            send(rows(other, (2 + c) * n, n), rows(other, (2 + c) * n, n), dev(dc=1)),
        ]

    proc_d(0, tok, 0)
    proc_g(0, tok, 0)
    c_share = share(0)
    f_cot = forward(c_cot, cot)
    proc_d(slot1, 2 * tok, 0)
    c_share += share(1)
    for cp in c_share:
        cp.wait_recv()
    transpose(cot, cot_t, 0)
    c_share2 = share(2)
    f_mix = forward(c_mix, mix)
    proc_d(0, 3 * tok, 1)
    for cp in c_share2:
        cp.wait_recv()
    proc_g(0, tok, 1)
    proc_g(slot1, 2 * tok, 0)
    proc_g(slot1, 2 * tok, 1)
    transpose(mix, mix_t, 0)
    back(0, 3 * tok)
    outp(0, 3 * tok)
    for cp in f_cot:
        cp.wait_recv()
    proc_d(slot3, tok, 0)
    proc_d(slot3, tok, 1)
    transpose(cot, cot_t, 1)
    for cp in f_mix:
        cp.wait_recv()

    def spread3(part, far):
        return [
            send(rows(part, slot3, half), far.at[0], dev(dx=-1)),
            send(rows(part, slot3 + half, half), far.at[1], dev(dx=1)),
        ]

    def spread1(part, near):
        return [
            send(rows(part, slot1 + half, half), near.at[0, pl.ds(half, half)], dev(dx=-1)),
            send(rows(part, slot2, half), near.at[1, pl.ds(0, half)], dev(dx=1)),
        ]

    def merge(part, far, copies, near):
        copies[0].wait_recv()
        r = pl.ds(slot1, half)
        part[r, :] = (part[r, :].astype(F32) + far[0].astype(F32)).astype(BF16)
        a = send(rows(part, slot1, half), near.at[0, pl.ds(0, half)], dev(dx=-1))
        copies[1].wait_recv()
        r = pl.ds(slot2 + half, half)
        part[r, :] = (part[r, :].astype(F32) + far[1].astype(F32)).astype(BF16)
        b = send(rows(part, slot2 + half, half), near.at[1, pl.ds(half, half)], dev(dx=1))
        return [a, b]

    def weight_grad(g, lhs, rhs):
        cp = None
        for cc in (1 - c, c):
            for h in range(2):
                yl2 = yl if h == 0 else 1 - yl
                v = mm(lhs[cc], rhs[:, pl.ds(h * ff, ff)]) * grad_scale
                for yh2 in range(2):
                    gb[g, cc, yh2 * 2 + yl2] = v[yh2 * 256 : yh2 * 256 + 256].astype(BF16)
            if cp is None:
                cp = send(gb.at[g, cc], rc.at[g], dev(dc=1))
        return cp

    def add_core(g, cp):
        cp.wait_recv()
        for t in range(NY):
            gb[g, c, t] = (gb[g, c, t].astype(F32) + rc[g, t].astype(F32)).astype(BF16)

    yup, ydown, yfar = lax.rem(y + 1, NY), lax.rem(y + 3, NY), lax.rem(y + 2, NY)
    n_y = gb.shape[3]
    h_y = n_y // 2

    def y_first(g):
        lo, hi = pl.ds(0, h_y), pl.ds(h_y, h_y)
        far = [
            send(gb.at[g, c, yfar, lo], ry2.at[g, 0], dev(dy=-1)),
            send(gb.at[g, c, yfar, hi], ry2.at[g, 1], dev(dy=1)),
        ]
        near = [
            send(gb.at[g, c, ydown, hi], ry1.at[g, 0, hi], dev(dy=-1)),
            send(gb.at[g, c, yup, lo], ry1.at[g, 1, lo], dev(dy=1)),
        ]
        return far, near

    def y_merge(g, cps):
        far, near = cps
        lo, hi = pl.ds(0, h_y), pl.ds(h_y, h_y)
        far[0].wait_recv()
        gb[g, c, ydown, lo] = (gb[g, c, ydown, lo].astype(F32) + ry2[g, 0].astype(F32)).astype(BF16)
        near.append(send(gb.at[g, c, ydown, lo], ry1.at[g, 0, lo], dev(dy=-1)))
        far[1].wait_recv()
        gb[g, c, yup, hi] = (gb[g, c, yup, hi].astype(F32) + ry2[g, 1].astype(F32)).astype(BF16)
        near.append(send(gb.at[g, c, yup, hi], ry1.at[g, 1, hi], dev(dy=1)))
        return near

    def y_last(g, near):
        for cp in near:
            cp.wait_recv()
        v = gb[g, c, y].astype(F32) + ry1[g, 0].astype(F32) + ry1[g, 1].astype(F32)
        gz[g] = v.astype(BF16).reshape(NZ, 32, ff)
        return [
            send(gz.at[g, lax.rem(z + d, NZ)], rz.at[g, d - 1], dev(dz=d))
            for d in (4, 3, 5, 2, 6, 1, 7)
        ]

    def z_last(g, cps, out):
        for cp in cps:
            cp.wait_recv()
        v = gz[g, z].astype(F32)
        for d in range(NZ - 1):
            v = v + rz[g, d].astype(F32)
        out[...] = v

    def stripe(d, r0, n):
        return pl.ds(pl.multiple_of(lax.rem(z + d + NZ, NZ) * 32 + r0, 16), n)

    def z_step(k, cps):
        new = []
        for way, sign in ((0, 1), (1, -1)):
            if k == 1:
                st = stripe(4, way * 16, 16)
                new.append(send(gb.at[2, c, :, st], zr.at[way, 0, :, pl.ds(way * 16, 16)], dev(dz=sign)))
                continue
            cps[way].wait_recv()
            if k == 2:
                st, r = stripe(3 * sign, way * 16, 16), pl.ds(way * 16, 16)
            else:
                st, r = stripe((5 - k) * sign, 0, 32), pl.ds(0, 32)
            gb[2, c, :, st] = (gb[2, c, :, st].astype(F32) + zr[way, k - 2, :, r].astype(F32)).astype(BF16)
            st = stripe((5 - k) * sign, 0, 32)
            new.append(send(gb.at[2, c, :, st], zr.at[way, k - 1], dev(dz=sign)))
        return new

    def z_done(cps):
        for cp in cps:
            cp.wait_recv()
        st = stripe(0, 0, 32)
        v = gb[2, c, :, st].astype(F32) + zr[0, 3].astype(F32) + zr[1, 3].astype(F32)
        gy[...] = v.astype(BF16)
        return [
            send(gy.at[lax.rem(y + d, NY)], rzy.at[d - 1], dev(dy=d)) for d in range(1, NY)
        ]

    def zy_last(cps, out):
        for cp in cps:
            cp.wait_recv()
        v = gy[y].astype(F32)
        for d in range(NY - 1):
            v = v + rzy[d].astype(F32)
        out[...] = v

    def total(part, near, copies, store):
        for cp in copies:
            cp.wait_recv()
        for j in range(4):
            r = pl.ds(j * lat, lat)
            v = part[r, :].astype(F32) + near[0, r, :].astype(F32) + near[1, r, :].astype(F32)
            store(j, v.astype(BF16))

    def store_dm(j, v):
        dm[j] = v

    def kernel_tile(e):
        cs = pl.ds(e * 128, 128)
        cols = [halo[0, :, cs]] + [f_ref[j, :, cs] for j in range(4)] + [halo[1, :, cs]]
        cols = [v.astype(F32) for v in cols]
        sums = [None] * 9
        for j in range(4):
            d = dm[j, :, cs].astype(F32)
            for a, v in enumerate((up(d), d, down(d))):
                for b in range(3):
                    p = v * cols[j + b]
                    i = 3 * a + b
                    sums[i] = p if sums[i] is None else sums[i] + p
        for i in range(9):
            kp[e, pl.ds(i, 1), :] = jnp.sum(sums[i], axis=0, keepdims=True) * grad_scale

    me = 2 * x + c

    def kernel_terms():
        kp[...] = jnp.zeros(kp.shape, F32)
        for e in range(NX * NC):
            kernel_tile(e)
        cps = []
        for i, (dx, dc) in enumerate(squad):
            to = 2 * lax.rem(x + dx, NX) + lax.rem(c + dc, NC)
            cps.append(send(kp.at[to], rk1.at[i], dev(dx=dx, dc=dc)))
        return cps

    def kernel_y(cps):
        for cp in cps:
            cp.wait_recv()
        v = kp[me]
        for i in range(len(squad)):
            v = v + rk1[i]
        rk2[y] = v
        return [send(rk2.at[y], rk2.at[y], dev(dy=d)) for d in range(1, NY)]

    def kernel_z(cps):
        for cp in cps:
            cp.wait_recv()
        rk3[z] = rk2[0] + rk2[1] + rk2[2] + rk2[3]
        return [send(rk3.at[z], rk3.at[z], dev(dz=d)) for d in range(1, NZ)]

    def kernel_all(cps):
        for cp in cps:
            cp.wait_recv()
        v = rk3[0]
        for i in range(1, NZ):
            v = v + rk3[i]
        kf[me] = v
        return [send(kf.at[me], kf.at[me], dev(dx=dx, dc=dc)) for dx, dc in squad]

    def kernel_last(cps):
        for cp in cps:
            cp.wait_recv()
        for e in range(NX * NC):
            for a in range(3):
                for b in range(3):
                    o_gk[a, pl.ds(b, 1), pl.ds(e * 128, 128)] = kf[e, pl.ds(3 * a + b, 1), :]

    def store_in(j, cs, v):
        o_in[j, :, cs] = v

    def store_out(j, v):
        o_out[pl.ds(j * lat, lat), :] = v

    c_b1 = spread1(pb, rb1)
    proc_g(slot3, tok, 0)
    proc_g(slot3, tok, 1)
    back(slot3, tok)
    c_b3 = spread3(pb, rb3)
    transpose(mix, mix_t, 1)
    g2 = weight_grad(2, cot_t, hid)
    g0 = weight_grad(0, mix_t, dg)
    outp(slot3, tok)
    g1 = weight_grad(1, mix_t, du)
    add_core(2, g2)
    zc = z_step(1, None)
    c_b1 += merge(pb, rb3, c_b3, rb1)
    c_o3 = spread3(po, ro3)
    add_core(0, g0)
    y0 = y_first(0)
    c_o1 = spread1(po, ro1)
    zc = z_step(2, zc)
    add_core(1, g1)
    y1 = y_first(1)
    c_o1 += merge(po, ro3, c_o3, ro1)
    total(pb, rb1, c_b1, store_dm)
    c_dh = [send(dm.at[3], dhalo.at[0], lon_up), send(dm.at[0], dhalo.at[1], lon_down)]
    c_k = kernel_terms()
    y0 = y_merge(0, y0)
    zc = z_step(3, zc)
    c_k = kernel_y(c_k)
    for cp in c_dh:
        cp.wait_recv()
    conv(dm, dhalo, True, store_in)
    y1 = y_merge(1, y1)
    zc = z_step(4, zc)
    c_k = kernel_z(c_k)
    z0 = y_last(0, y0)
    c_k = kernel_all(c_k)
    zy = z_done(zc)
    total(po, ro1, c_o1, store_out)
    z1 = y_last(1, y1)
    z_last(0, z0, o_gg)
    kernel_last(c_k)
    zy_last(zy, o_gd)
    z_last(1, z1, o_gu)
    for cp in started:
        cp.wait_send()


def place(*refs):
    for i, (src, dst) in enumerate(zip(refs[:6], refs[6:])):
        dst[...] = jnp.swapaxes(src[...], 0, 1) if i < 2 else src[...]


def shards(fields, conv_kernel, gate_weight, up_weight, down_weight, cotangent):
    _, lat, lon, width = fields.shape
    ff = gate_weight.shape[1]
    tok = lat * lon
    total_tokens = tok * lax.axis_size("shard") * lax.axis_size("lon")
    grad_scale = 1.0 / float(total_tokens) ** 0.5
    rows_d = width // 32
    vmem = lambda *shape, dtype=BF16: pltpu.VMEM(shape, dtype)
    call = pl.pallas_call(
        lambda *refs: kernel(grad_scale, *refs),
        name="swiglu_block",
        out_shape=[
            jax.ShapeDtypeStruct((tok, width), BF16),
            jax.ShapeDtypeStruct((lon, lat, width), BF16),
            jax.ShapeDtypeStruct((rows_d, ff), F32),
            jax.ShapeDtypeStruct((rows_d, ff), F32),
            jax.ShapeDtypeStruct((rows_d, ff), F32),
            jax.ShapeDtypeStruct((3, 3, width), F32),
        ],
        in_specs=[pl.BlockSpec(memory_space=pltpu.VMEM if i == 1 else pl.ANY) for i in range(6)],
        out_specs=[pl.BlockSpec(memory_space=pltpu.VMEM)] * 6,
        scratch_shapes=[
            vmem(lat, lon, width),
            vmem(lat, lon, width),
            vmem(lon, lat, width),
            vmem(width, ff),
            vmem(width, ff),
            vmem(ff, width),
            vmem(2, lat, width),
            vmem(2, lat, width),
            vmem(width, ff),
            vmem(width, ff),
            vmem(ff, width),
            vmem(4 * tok, width),
            vmem(4 * tok, width),
            vmem(4 * tok, 2 * ff),
            vmem(4 * tok, 2 * ff),
            vmem(4 * tok, 2 * ff),
            vmem(4 * tok, width),
            vmem(4 * tok, width),
            vmem(2, tok // 2, width),
            vmem(2, tok, width),
            vmem(2, tok // 2, width),
            vmem(2, tok, width),
            vmem(4 * tok, 2 * ff, dtype=F32),
            vmem(2, width // 2, 4 * tok),
            vmem(2, width // 2, 4 * tok),
            vmem(3, 2, NY, width // 4, ff),
            vmem(3, NY, width // 4, ff),
            vmem(2, 2, width // 8, ff),
            vmem(2, 2, width // 4, ff),
            vmem(2, NZ, 32, ff),
            vmem(2, NZ - 1, 32, ff),
            vmem(2, 4, NY, 32, ff),
            vmem(NY, 32, ff),
            vmem(NY - 1, 32, ff),
            vmem(lon, lat, width),
            vmem(8, 16, width // 8, dtype=F32),
            vmem(7, 16, width // 8, dtype=F32),
            vmem(NY, 16, width // 8, dtype=F32),
            vmem(NZ, 16, width // 8, dtype=F32),
            vmem(8, 16, width // 8, dtype=F32),
            pltpu.SemaphoreType.DMA((N_SEM,)),
            pltpu.SemaphoreType.DMA((N_SEM,)),
            pltpu.SemaphoreType.DMA((5,)),
        ],
        compiler_params=pltpu.CompilerParams(
            collective_id=0, has_side_effects=True, vmem_limit_bytes=60 * 2**20
        ),
        cost_estimate=pl.CostEstimate(flops=14_500_000_000, bytes_accessed=6_000_000, transcendentals=800_000),
    )
    out, in_grad, gg, gu, gd, gk = call(
        fields[0], conv_kernel, gate_weight, up_weight, down_weight, cotangent[0]
    )

    results = (out.reshape(lon, lat, width), in_grad, gg, gu, gd, gk)
    grid_shape = jax.ShapeDtypeStruct((lat, lon, width), BF16)
    out, in_grad, gg, gu, gd, gk = pl.pallas_call(
        place,
        name="place",
        out_shape=[grid_shape] * 2 + [jax.ShapeDtypeStruct(v.shape, v.dtype) for v in results[2:]],
        in_specs=[pl.BlockSpec(memory_space=pltpu.VMEM)] * 6,
        out_specs=[pl.BlockSpec(memory_space=pltpu.VMEM)] * 6,
    )(*results)
    return out[None], in_grad[None], gg, gu, gd.T, gk


def solution(mesh):
    placed = (
        P("shard", None, "lon", None),
        P(),
        P(None, "shard"),
        P(None, "shard"),
        P("shard", None),
        P("shard", None, "lon", None),
    )
    return jax.shard_map(
        shards,
        mesh=mesh,
        in_specs=placed,
        out_specs=(
            P("shard", None, "lon", None),
            P("shard", None, "lon", None),
            P("lon", "shard"),
            P("lon", "shard"),
            P("shard", "lon"),
            P(),
        ),
        check_vma=False,
    )
```

```python
import jax
import jax.numpy as jnp
from jax import lax
from jax.experimental import pallas as pl
from jax.experimental.pallas import tpu as pltpu
from jax.sharding import PartitionSpec as P

MESH = pl.DeviceIdType.MESH
F32, BF16 = jnp.float32, jnp.bfloat16
NX, NY, NZ, NC = 4, 4, 8, 2
NN = (((1,), (0,)), ((), ()))
NT = (((1,), (1,)), ((), ()))
N_SEM = 160


def mm(a, b, dims=NN):
    return lax.dot_general(a, b, dims, preferred_element_type=F32)


def kernel(
    grad_scale, f_in, k_ref, wg_in, wu_in, wd_in, t_in,
    o_out, o_in, o_gg, o_gu, o_gd, o_gk,
    f_raw, t_raw, f_ref, wg, wu, wd, halo, dhalo, wg2, wu2, wd2, mix, cot, hid, dg, du, pb, po, rb3, rb1, ro3, ro1,
    dh, mix_t, cot_t, gb, rc, ry2, ry1, gz, rz, zr, gy, rzy, dm, kp, rk1, rk2, rk3, kf, ssem, rsem, lsem,
):
    width, lat = f_ref.shape[2], f_ref.shape[1]
    local = [
        pltpu.make_async_copy(src, dst, lsem.at[i])
        for i, (src, dst) in enumerate((
            (f_in, f_raw), (t_in, t_raw), (wd_in, wd), (wg_in, wg), (wu_in, wu),
        ))
    ]
    for cp in local:
        cp.start()
    tok = 4 * lat
    half = tok // 2
    ff = wg.shape[1]
    cols_u = ff // 2
    s, l = lax.axis_index("shard"), lax.axis_index("lon")
    x, yl = lax.rem(s, 4), s // 4
    z, yh, c = l // 4, lax.rem(l // 2, 2), lax.rem(l, 2)
    y = yh * 2 + yl

    def dev(dx=0, dy=0, dz=0, dc=0):
        x2 = lax.rem(x + dx + NX, NX)
        y2 = lax.rem(y + dy + NY, NY)
        z2 = lax.rem(z + dz + NZ, NZ)
        c2 = lax.rem(c + dc, NC)
        return (lax.rem(y2, 2) * 4 + x2, z2 * 4 + (y2 // 2) * 2 + c2)

    lon_up = (s, lax.rem(l + 1, 32))
    lon_down = (s, lax.rem(l + 31, 32))
    squad = [(dx, dc) for dx in range(NX) for dc in range(NC) if (dx, dc) != (0, 0)]
    partners = [dev(dx=dx, dc=dc) for dx, dc in squad]
    partners += [dev(dy=d) for d in range(1, NY)]
    partners += [dev(dz=d) for d in range(1, NZ)]
    partners += [lon_up, lon_down]

    barrier = pltpu.get_barrier_semaphore()
    for p in partners:
        pl.semaphore_signal(barrier, inc=1, device_id=p, device_id_type=MESH)
    pl.semaphore_wait(barrier, len(partners))

    started = []

    def send(src, dst, to):
        i = len(started)
        copy = pltpu.make_async_remote_copy(
            src_ref=src, dst_ref=dst, send_sem=ssem.at[i], recv_sem=rsem.at[i],
            device_id=to, device_id_type=MESH,
        )
        copy.start()
        started.append(copy)
        return copy

    def rows(ref, r0, n):
        return ref.at[pl.ds(r0, n)]

    local[0].wait()
    f_ref[...] = jnp.swapaxes(f_raw[...], 0, 1)
    c_halo = [send(f_ref.at[3], halo.at[0], lon_up), send(f_ref.at[0], halo.at[1], lon_down)]
    slot1, slot2, slot3 = tok, 2 * tok, 3 * tok
    local[1].wait()
    cot[pl.ds(0, tok), :] = jnp.swapaxes(t_raw[...], 0, 1).reshape(tok, width)
    c_cot = [
        send(rows(cot, 0, tok), rows(cot, slot1, tok), dev(dx=1)),
        send(rows(cot, 0, tok), rows(cot, slot2, tok), dev(dx=-1)),
    ]
    c_w = []
    for i, (own, other) in enumerate(((wd, wd2), (wg, wg2), (wu, wu2))):
        local[2 + i].wait()
        n = own.shape[0] // 4
        q_up, q_down = rows(own, c * n, n), rows(own, (2 + c) * n, n)
        c_w.append((
            send(q_up, rows(other, c * n, n), dev(dy=1)),
            send(q_down, rows(other, (2 + c) * n, n), dev(dy=-1)),
            other, n,
        ))

    row = lax.broadcasted_iota(jnp.int32, (lat, 128), 0)

    def down(v):
        return jnp.where(row == 0, 0.0, pltpu.roll(v, 1, 0))

    def up(v):
        return jnp.where(row == lat - 1, 0.0, pltpu.roll(v, lat - 1, 0))

    def conv(src, edges, flip, store):
        for t in range(width // 128):
            cs = pl.ds(t * 128, 128)
            cols = [edges[0, :, cs]] + [src[j, :, cs] for j in range(4)] + [edges[1, :, cs]]
            cols = [v.astype(F32) for v in cols]
            taps = [
                k_ref[2 - a if flip else a, 2 - b if flip else b, cs].reshape(1, 128)
                for a in range(3) for b in range(3)
            ]
            for j in range(4):
                a0, a1, a2 = (
                    sum(taps[3 * a + b] * cols[j + b] for b in range(3)) for a in range(3)
                )
                store(j, cs, (cols[j + 1] + a1 + down(a0) + up(a2)).astype(BF16))

    for cp in c_halo:
        cp.wait_recv()

    def store_mixed(j, cs, v):
        mix[pl.ds(j * lat, lat), cs] = v

    conv(f_ref, halo, False, store_mixed)
    c_mix = [
        send(rows(mix, 0, tok), rows(mix, slot1, tok), dev(dx=1)),
        send(rows(mix, 0, tok), rows(mix, slot2, tok), dev(dx=-1)),
    ]

    def transpose(src, dst, pair):
        r = pl.ds(pair * 2 * tok, 2 * tok)
        for b in range(width // 128):
            v = src[r, pl.ds(b * 128, 128)].T
            for q in range(4):
                dst[q % 2, pl.ds(q // 2 * 256 + b * 32, 32), r] = v[q * 32 : q * 32 + 32]

    weights = ((wg, wu, wd), (wg2, wu2, wd2))

    def proc_d(r0, n, h):
        wdr = weights[h][2]
        dh[pl.ds(r0, n), pl.ds(h * ff, ff)] = mm(cot[pl.ds(r0, n), :], wdr[...], NT)

    def proc_g(r0, n, h):
        wgr, wur, _ = weights[h]
        r = pl.ds(r0, n)
        for t in range(ff // 256):
            cs = pl.ds(t * 256, 256)
            oc = pl.ds(h * ff + t * 256, 256)
            gate = mm(mix[r, :], wgr[:, cs])
            value = mm(mix[r, :], wur[:, cs])
            dhid = dh[r, oc]
            sig = 1.0 / (1.0 + jnp.exp(-gate))
            act = gate * sig
            hid[r, oc] = (act * value).astype(BF16)
            dg[r, oc] = (dhid * value * sig * (1.0 + gate * (1.0 - sig))).astype(BF16)
            du[r, oc] = (dhid * act).astype(BF16)

    def back(r0, n):
        r = pl.ds(r0, n)
        for t in range(width // 512):
            cs = pl.ds(t * 512, 512)
            acc = None
            for h in range(2):
                wgr, wur, _ = weights[h]
                hs = pl.ds(h * ff, ff)
                a = mm(dg[r, hs], wgr[cs, :], NT) + mm(du[r, hs], wur[cs, :], NT)
                acc = a if acc is None else acc + a
            pb[r, cs] = acc.astype(BF16)

    def outp(r0, n):
        r = pl.ds(r0, n)
        for t in range(width // 512):
            cs = pl.ds(t * 512, 512)
            acc = mm(hid[r, pl.ds(0, ff)], wd[:, cs]) + mm(hid[r, pl.ds(ff, ff)], wd2[:, cs])
            po[r, cs] = acc.astype(BF16)

    def forward(copies, buf):
        copies[0].wait_recv()
        a = send(rows(buf, slot1, half), rows(buf, slot3, half), dev(dx=1))
        copies[1].wait_recv()
        b = send(rows(buf, slot2 + half, half), rows(buf, slot3 + half, half), dev(dx=-1))
        return [a, b]

    def share(i):
        cu, cd, other, n = c_w[i]
        cu.wait_recv()
        cd.wait_recv()
        return [
            send(rows(other, c * n, n), rows(other, c * n, n), dev(dc=1)),
            send(rows(other, (2 + c) * n, n), rows(other, (2 + c) * n, n), dev(dc=1)),
        ]

    proc_d(0, tok, 0)
    proc_g(0, tok, 0)
    c_share = share(0)
    f_cot = forward(c_cot, cot)
    proc_d(slot1, 2 * tok, 0)
    c_share += share(1)
    for cp in c_share:
        cp.wait_recv()
    transpose(cot, cot_t, 0)
    c_share2 = share(2)
    f_mix = forward(c_mix, mix)
    proc_d(0, 3 * tok, 1)
    for cp in c_share2:
        cp.wait_recv()
    proc_g(0, tok, 1)
    proc_g(slot1, 2 * tok, 0)
    proc_g(slot1, 2 * tok, 1)
    transpose(mix, mix_t, 0)
    back(0, 3 * tok)
    outp(0, 3 * tok)
    for cp in f_cot:
        cp.wait_recv()
    proc_d(slot3, tok, 0)
    proc_d(slot3, tok, 1)
    transpose(cot, cot_t, 1)
    for cp in f_mix:
        cp.wait_recv()

    def spread3(part, far):
        return [
            send(rows(part, slot3, half), far.at[0], dev(dx=-1)),
            send(rows(part, slot3 + half, half), far.at[1], dev(dx=1)),
        ]

    def spread1(part, near):
        return [
            send(rows(part, slot1 + half, half), near.at[0, pl.ds(half, half)], dev(dx=-1)),
            send(rows(part, slot2, half), near.at[1, pl.ds(0, half)], dev(dx=1)),
        ]

    def merge(part, far, copies, near):
        copies[0].wait_recv()
        r = pl.ds(slot1, half)
        part[r, :] = (part[r, :].astype(F32) + far[0].astype(F32)).astype(BF16)
        a = send(rows(part, slot1, half), near.at[0, pl.ds(0, half)], dev(dx=-1))
        copies[1].wait_recv()
        r = pl.ds(slot2 + half, half)
        part[r, :] = (part[r, :].astype(F32) + far[1].astype(F32)).astype(BF16)
        b = send(rows(part, slot2 + half, half), near.at[1, pl.ds(half, half)], dev(dx=1))
        return [a, b]

    def weight_grad(g, u, lhs, rhs):
        cp = None
        for cc in (1 - c, c):
            for h in range(2):
                yl2 = yl if h == 0 else 1 - yl
                v = mm(lhs[cc], rhs[:, pl.ds(h * ff + u * cols_u, cols_u)]) * grad_scale
                for yh2 in range(2):
                    gb[g, cc, u, yh2 * 2 + yl2] = v[yh2 * 256 : yh2 * 256 + 256].astype(BF16)
            if cp is None:
                cp = send(gb.at[g, cc, u], rc.at[g, u], dev(dc=1))
        return cp

    def add_core(g, u, cp):
        cp.wait_recv()
        for t in range(NY):
            gb[g, c, u, t] = (gb[g, c, u, t].astype(F32) + rc[g, u, t].astype(F32)).astype(BF16)

    yup, ydown, yfar = lax.rem(y + 1, NY), lax.rem(y + 3, NY), lax.rem(y + 2, NY)
    n_y = gb.shape[4]
    lo, hi = pl.ds(0, n_y // 2), pl.ds(n_y // 2, n_y // 2)

    def y_first(g, u):
        far = [
            send(gb.at[g, c, u, yfar, lo], ry2.at[g, u, 0], dev(dy=-1)),
            send(gb.at[g, c, u, yfar, hi], ry2.at[g, u, 1], dev(dy=1)),
        ]
        near = [
            send(gb.at[g, c, u, ydown, hi], ry1.at[g, u, 0, hi], dev(dy=-1)),
            send(gb.at[g, c, u, yup, lo], ry1.at[g, u, 1, lo], dev(dy=1)),
        ]
        return far, near

    def y_merge(g, u, cps):
        far, near = cps
        for i, (to, part, sign) in enumerate(((ydown, lo, -1), (yup, hi, 1))):
            far[i].wait_recv()
            v = gb[g, c, u, to, part].astype(F32) + ry2[g, u, i].astype(F32)
            gb[g, c, u, to, part] = v.astype(BF16)
            near.append(send(gb.at[g, c, u, to, part], ry1.at[g, u, i, part], dev(dy=sign)))
        return near

    def y_last(g, u, near):
        for cp in near:
            cp.wait_recv()
        v = gb[g, c, u, y].astype(F32) + ry1[g, u, 0].astype(F32) + ry1[g, u, 1].astype(F32)
        gz[g, u] = v.astype(BF16).reshape(NZ, 32, cols_u)
        return [
            send(gz.at[g, u, lax.rem(z + d, NZ)], rz.at[g, u, d - 1], dev(dz=d))
            for d in (4, 3, 5, 2, 6, 1, 7)
        ]

    def z_last(g, u, cps, out):
        for cp in cps:
            cp.wait_recv()
        v = gz[g, u, z].astype(F32)
        for d in range(NZ - 1):
            v = v + rz[g, u, d].astype(F32)
        out[:, pl.ds(u * cols_u, cols_u)] = v

    def stripe(d, r0, n):
        return pl.ds(pl.multiple_of(lax.rem(z + d + NZ, NZ) * 32 + r0, 16), n)

    def z_step(k, u, cps):
        new = []
        for way, sign in ((0, 1), (1, -1)):
            if k == 1:
                st, r = stripe(4, way * 16, 16), pl.ds(way * 16, 16)
                new.append(send(gb.at[2, c, u, :, st], zr.at[u, way, 0, :, r], dev(dz=sign)))
                continue
            cps[way].wait_recv()
            if k == 2:
                st, r = stripe(3 * sign, way * 16, 16), pl.ds(way * 16, 16)
            else:
                st, r = stripe((5 - k) * sign, 0, 32), pl.ds(0, 32)
            v = gb[2, c, u, :, st].astype(F32) + zr[u, way, k - 2, :, r].astype(F32)
            gb[2, c, u, :, st] = v.astype(BF16)
            st = stripe((5 - k) * sign, 0, 32)
            new.append(send(gb.at[2, c, u, :, st], zr.at[u, way, k - 1], dev(dz=sign)))
        return new

    def z_done(u, cps):
        for cp in cps:
            cp.wait_recv()
        st = stripe(0, 0, 32)
        v = gb[2, c, u, :, st].astype(F32) + zr[u, 0, 3].astype(F32) + zr[u, 1, 3].astype(F32)
        gy[u] = v.astype(BF16)
        return [
            send(gy.at[u, lax.rem(y + d, NY)], rzy.at[u, d - 1], dev(dy=d)) for d in range(1, NY)
        ]

    def zy_last(u, cps, out):
        for cp in cps:
            cp.wait_recv()
        v = gy[u, y].astype(F32)
        for d in range(NY - 1):
            v = v + rzy[u, d].astype(F32)
        out[:, pl.ds(u * cols_u, cols_u)] = v

    def total(part, near, copies, store):
        for cp in copies:
            cp.wait_recv()
        for j in range(4):
            r = pl.ds(j * lat, lat)
            v = part[r, :].astype(F32) + near[0, r, :].astype(F32) + near[1, r, :].astype(F32)
            store(j, v.astype(BF16))

    def store_dm(j, v):
        dm[j] = v

    def kernel_tile(e):
        cs = pl.ds(e * 128, 128)
        cols = [halo[0, :, cs]] + [f_ref[j, :, cs] for j in range(4)] + [halo[1, :, cs]]
        cols = [v.astype(F32) for v in cols]
        sums = [None] * 9
        for j in range(4):
            d = dm[j, :, cs].astype(F32)
            for a, v in enumerate((up(d), d, down(d))):
                for b in range(3):
                    p = v * cols[j + b]
                    i = 3 * a + b
                    sums[i] = p if sums[i] is None else sums[i] + p
        for i in range(9):
            kp[e, pl.ds(i, 1), :] = jnp.sum(sums[i], axis=0, keepdims=True) * grad_scale

    me = 2 * x + c

    def kernel_terms():
        kp[...] = jnp.zeros(kp.shape, F32)
        for e in range(NX * NC):
            kernel_tile(e)
        cps = []
        for i, (dx, dc) in enumerate(squad):
            to = 2 * lax.rem(x + dx, NX) + lax.rem(c + dc, NC)
            cps.append(send(kp.at[to], rk1.at[i], dev(dx=dx, dc=dc)))
        return cps

    def kernel_y(cps):
        for cp in cps:
            cp.wait_recv()
        v = kp[me]
        for i in range(len(squad)):
            v = v + rk1[i]
        rk2[y] = v
        return [send(rk2.at[y], rk2.at[y], dev(dy=d)) for d in range(1, NY)]

    def kernel_z(cps):
        for cp in cps:
            cp.wait_recv()
        rk3[z] = rk2[0] + rk2[1] + rk2[2] + rk2[3]
        return [send(rk3.at[z], rk3.at[z], dev(dz=d)) for d in range(1, NZ)]

    def kernel_all(cps):
        for cp in cps:
            cp.wait_recv()
        v = rk3[0]
        for i in range(1, NZ):
            v = v + rk3[i]
        kf[me] = v
        return [send(kf.at[me], kf.at[me], dev(dx=dx, dc=dc)) for dx, dc in squad]

    def kernel_last(cps):
        for cp in cps:
            cp.wait_recv()
        for e in range(NX * NC):
            for a in range(3):
                for b in range(3):
                    o_gk[a, pl.ds(b, 1), pl.ds(e * 128, 128)] = kf[e, pl.ds(3 * a + b, 1), :]

    def store_in(j, cs, v):
        o_in[j, :, cs] = v

    def store_out(j, v):
        o_out[pl.ds(j * lat, lat), :] = v

    c_b1 = spread1(pb, rb1)
    proc_g(slot3, tok, 0)
    proc_g(slot3, tok, 1)
    back(slot3, tok)
    c_b3 = spread3(pb, rb3)
    transpose(mix, mix_t, 1)
    g00 = weight_grad(0, 0, mix_t, dg)
    g20 = weight_grad(2, 0, cot_t, hid)
    g01 = weight_grad(0, 1, mix_t, dg)
    add_core(0, 0, g00)
    y00 = y_first(0, 0)
    g21 = weight_grad(2, 1, cot_t, hid)
    add_core(2, 0, g20)
    za = z_step(1, 0, None)
    g10 = weight_grad(1, 0, mix_t, du)
    add_core(0, 1, g01)
    y01 = y_first(0, 1)
    g11 = weight_grad(1, 1, mix_t, du)
    c_b1 += merge(pb, rb3, c_b3, rb1)
    add_core(2, 1, g21)
    zb = z_step(1, 1, None)
    y00 = y_merge(0, 0, y00)
    za = z_step(2, 0, za)
    outp(slot3, tok)
    c_o3 = spread3(po, ro3)
    add_core(1, 0, g10)
    y10 = y_first(1, 0)
    zb = z_step(2, 1, zb)
    add_core(1, 1, g11)
    y11 = y_first(1, 1)
    c_o1 = spread1(po, ro1)
    y01 = y_merge(0, 1, y01)
    za = z_step(3, 0, za)
    total(pb, rb1, c_b1, store_dm)
    c_dh = [send(dm.at[3], dhalo.at[0], lon_up), send(dm.at[0], dhalo.at[1], lon_down)]
    c_k = kernel_terms()
    y00 = y_last(0, 0, y00)
    zb = z_step(3, 1, zb)
    y10 = y_merge(1, 0, y10)
    za = z_step(4, 0, za)
    c_k = kernel_y(c_k)
    y11 = y_merge(1, 1, y11)
    y01 = y_last(0, 1, y01)
    zb = z_step(4, 1, zb)
    c_o1 += merge(po, ro3, c_o3, ro1)
    c_k = kernel_z(c_k)
    for cp in c_dh:
        cp.wait_recv()
    conv(dm, dhalo, True, store_in)
    za = z_done(0, za)
    y10 = y_last(1, 0, y10)
    c_k = kernel_all(c_k)
    y11 = y_last(1, 1, y11)
    zb = z_done(1, zb)
    z_last(0, 0, y00, o_gg)
    z_last(0, 1, y01, o_gg)
    total(po, ro1, c_o1, store_out)
    kernel_last(c_k)
    zy_last(0, za, o_gd)
    z_last(1, 0, y10, o_gu)
    zy_last(1, zb, o_gd)
    z_last(1, 1, y11, o_gu)
    for cp in started:
        cp.wait_send()


def place(*refs):
    for i, (src, dst) in enumerate(zip(refs[:6], refs[6:])):
        dst[...] = jnp.swapaxes(src[...], 0, 1) if i < 2 else src[...]


def shards(fields, conv_kernel, gate_weight, up_weight, down_weight, cotangent):
    _, lat, lon, width = fields.shape
    ff = gate_weight.shape[1]
    tok = lat * lon
    total_tokens = tok * lax.axis_size("shard") * lax.axis_size("lon")
    grad_scale = 1.0 / float(total_tokens) ** 0.5
    rows_d = width // 32
    vmem = lambda *shape, dtype=BF16: pltpu.VMEM(shape, dtype)
    call = pl.pallas_call(
        lambda *refs: kernel(grad_scale, *refs),
        name="swiglu_block",
        out_shape=[
            jax.ShapeDtypeStruct((tok, width), BF16),
            jax.ShapeDtypeStruct((lon, lat, width), BF16),
            jax.ShapeDtypeStruct((rows_d, ff), F32),
            jax.ShapeDtypeStruct((rows_d, ff), F32),
            jax.ShapeDtypeStruct((rows_d, ff), F32),
            jax.ShapeDtypeStruct((3, 3, width), F32),
        ],
        in_specs=[pl.BlockSpec(memory_space=pltpu.VMEM if i == 1 else pl.ANY) for i in range(6)],
        out_specs=[pl.BlockSpec(memory_space=pltpu.VMEM)] * 6,
        scratch_shapes=[
            vmem(lat, lon, width),
            vmem(lat, lon, width),
            vmem(lon, lat, width),
            vmem(width, ff),
            vmem(width, ff),
            vmem(ff, width),
            vmem(2, lat, width),
            vmem(2, lat, width),
            vmem(width, ff),
            vmem(width, ff),
            vmem(ff, width),
            vmem(4 * tok, width),
            vmem(4 * tok, width),
            vmem(4 * tok, 2 * ff),
            vmem(4 * tok, 2 * ff),
            vmem(4 * tok, 2 * ff),
            vmem(4 * tok, width),
            vmem(4 * tok, width),
            vmem(2, tok // 2, width),
            vmem(2, tok, width),
            vmem(2, tok // 2, width),
            vmem(2, tok, width),
            vmem(4 * tok, 2 * ff, dtype=F32),
            vmem(2, width // 2, 4 * tok),
            vmem(2, width // 2, 4 * tok),
            vmem(3, 2, 2, NY, width // 4, ff // 2),
            vmem(3, 2, NY, width // 4, ff // 2),
            vmem(2, 2, 2, width // 8, ff // 2),
            vmem(2, 2, 2, width // 4, ff // 2),
            vmem(2, 2, NZ, 32, ff // 2),
            vmem(2, 2, NZ - 1, 32, ff // 2),
            vmem(2, 2, 4, NY, 32, ff // 2),
            vmem(2, NY, 32, ff // 2),
            vmem(2, NY - 1, 32, ff // 2),
            vmem(lon, lat, width),
            vmem(8, 16, width // 8, dtype=F32),
            vmem(7, 16, width // 8, dtype=F32),
            vmem(NY, 16, width // 8, dtype=F32),
            vmem(NZ, 16, width // 8, dtype=F32),
            vmem(8, 16, width // 8, dtype=F32),
            pltpu.SemaphoreType.DMA((N_SEM,)),
            pltpu.SemaphoreType.DMA((N_SEM,)),
            pltpu.SemaphoreType.DMA((5,)),
        ],
        compiler_params=pltpu.CompilerParams(
            collective_id=0, has_side_effects=True, vmem_limit_bytes=60 * 2**20
        ),
        cost_estimate=pl.CostEstimate(flops=14_500_000_000, bytes_accessed=6_000_000, transcendentals=800_000),
    )
    out, in_grad, gg, gu, gd, gk = call(
        fields[0], conv_kernel, gate_weight, up_weight, down_weight, cotangent[0]
    )

    results = (out.reshape(lon, lat, width), in_grad, gg, gu, gd, gk)
    grid_shape = jax.ShapeDtypeStruct((lat, lon, width), BF16)
    out, in_grad, gg, gu, gd, gk = pl.pallas_call(
        place,
        name="place",
        out_shape=[grid_shape] * 2 + [jax.ShapeDtypeStruct(v.shape, v.dtype) for v in results[2:]],
        in_specs=[pl.BlockSpec(memory_space=pltpu.VMEM)] * 6,
        out_specs=[pl.BlockSpec(memory_space=pltpu.VMEM)] * 6,
    )(*results)
    return out[None], in_grad[None], gg, gu, gd.T, gk


def solution(mesh):
    placed = (
        P("shard", None, "lon", None),
        P(),
        P(None, "shard"),
        P(None, "shard"),
        P("shard", None),
        P("shard", None, "lon", None),
    )
    return jax.shard_map(
        shards,
        mesh=mesh,
        in_specs=placed,
        out_specs=(
            P("shard", None, "lon", None),
            P("shard", None, "lon", None),
            P("lon", "shard"),
            P("lon", "shard"),
            P("shard", "lon"),
            P(),
        ),
        check_vma=False,
    )
```

```python
import jax
import jax.numpy as jnp
from jax import lax
from jax.experimental import pallas as pl
from jax.experimental.pallas import tpu as pltpu
from jax.sharding import PartitionSpec as P

MESH = pl.DeviceIdType.MESH
F32, BF16 = jnp.float32, jnp.bfloat16
NX, NY, NZ, NC = 4, 4, 8, 2
NN = (((1,), (0,)), ((), ()))
NT = (((1,), (1,)), ((), ()))
N_SEM = 160


def mm(a, b, dims=NN):
    return lax.dot_general(a, b, dims, preferred_element_type=F32)


def kernel(
    grad_scale, f_in, k_ref, wg_in, wu_in, wd_in, t_in,
    h_out, h_in, h_gg, h_gu, h_gd, h_gk,
    o_out, o_in, o_gg, o_gu, o_gd, o_gk, tmp,
    f_raw, t_raw, f_ref, wg, wu, wd, halo, dhalo, wg2, wu2, wd2, mix, cot, hid, dg, du, pb, po, rb3, rb1, ro3, ro1,
    dh, mix_t, cot_t, gb, rc, ry2, ry1, gz, rz, zr, gy, rzy, dm, kp, rk1, rk2, rk3, kf, ssem, rsem, lsem,
):
    width, lat = f_ref.shape[2], f_ref.shape[1]
    local = [
        pltpu.make_async_copy(src, dst, lsem.at[i])
        for i, (src, dst) in enumerate((
            (t_in, t_raw), (f_in, f_raw), (wd_in, wd), (wg_in, wg), (wu_in, wu),
        ))
    ]
    for cp in local:
        cp.start()
    tok = 4 * lat
    half = tok // 2
    ff = wg.shape[1]
    cols_u = ff // 2
    s, l = lax.axis_index("shard"), lax.axis_index("lon")
    x, yl = lax.rem(s, 4), s // 4
    z, yh, c = l // 4, lax.rem(l // 2, 2), lax.rem(l, 2)
    y = yh * 2 + yl

    def dev(dx=0, dy=0, dz=0, dc=0):
        x2 = lax.rem(x + dx + NX, NX)
        y2 = lax.rem(y + dy + NY, NY)
        z2 = lax.rem(z + dz + NZ, NZ)
        c2 = lax.rem(c + dc, NC)
        return (lax.rem(y2, 2) * 4 + x2, z2 * 4 + (y2 // 2) * 2 + c2)

    lon_up = (s, lax.rem(l + 1, 32))
    lon_down = (s, lax.rem(l + 31, 32))
    squad = [(dx, dc) for dx in range(NX) for dc in range(NC) if (dx, dc) != (0, 0)]
    partners = [dev(dx=dx, dc=dc) for dx, dc in squad]
    partners += [dev(dy=d) for d in range(1, NY)]
    partners += [dev(dz=d) for d in range(1, NZ)]
    partners += [lon_up, lon_down]

    barrier = pltpu.get_barrier_semaphore()
    for p in partners:
        pl.semaphore_signal(barrier, inc=1, device_id=p, device_id_type=MESH)
    local[0].wait()
    cot[pl.ds(0, tok), :] = jnp.swapaxes(t_raw[...], 0, 1).reshape(tok, width)
    pl.semaphore_wait(barrier, len(partners))

    started = []

    def send(src, dst, to):
        i = len(started)
        copy = pltpu.make_async_remote_copy(
            src_ref=src, dst_ref=dst, send_sem=ssem.at[i], recv_sem=rsem.at[i],
            device_id=to, device_id_type=MESH,
        )
        copy.start()
        started.append(copy)
        return copy

    def rows(ref, r0, n):
        return ref.at[pl.ds(r0, n)]

    slot1, slot2, slot3 = tok, 2 * tok, 3 * tok
    c_cot = [
        send(rows(cot, 0, tok), rows(cot, slot1, tok), dev(dx=1)),
        send(rows(cot, 0, tok), rows(cot, slot2, tok), dev(dx=-1)),
    ]
    local[1].wait()
    f_ref[...] = jnp.swapaxes(f_raw[...], 0, 1)
    c_halo = [send(f_ref.at[3], halo.at[0], lon_up), send(f_ref.at[0], halo.at[1], lon_down)]
    c_w = []
    for i, (own, other) in enumerate(((wd, wd2), (wg, wg2), (wu, wu2))):
        local[2 + i].wait()
        n = own.shape[0] // 4
        q_up, q_down = rows(own, c * n, n), rows(own, (2 + c) * n, n)
        c_w.append((
            send(q_up, rows(other, c * n, n), dev(dy=1)),
            send(q_down, rows(other, (2 + c) * n, n), dev(dy=-1)),
            other, n,
        ))

    row = lax.broadcasted_iota(jnp.int32, (lat, 128), 0)

    def down(v):
        return jnp.where(row == 0, 0.0, pltpu.roll(v, 1, 0))

    def up(v):
        return jnp.where(row == lat - 1, 0.0, pltpu.roll(v, lat - 1, 0))

    def conv(src, edges, flip, store):
        for t in range(width // 128):
            cs = pl.ds(t * 128, 128)
            cols = [edges[0, :, cs]] + [src[j, :, cs] for j in range(4)] + [edges[1, :, cs]]
            cols = [v.astype(F32) for v in cols]
            taps = [
                k_ref[2 - a if flip else a, 2 - b if flip else b, cs].reshape(1, 128)
                for a in range(3) for b in range(3)
            ]
            for j in range(4):
                a0, a1, a2 = (
                    sum(taps[3 * a + b] * cols[j + b] for b in range(3)) for a in range(3)
                )
                store(j, cs, (cols[j + 1] + a1 + down(a0) + up(a2)).astype(BF16))

    for cp in c_halo:
        cp.wait_recv()

    def store_mixed(j, cs, v):
        mix[pl.ds(j * lat, lat), cs] = v

    conv(f_ref, halo, False, store_mixed)
    c_mix = [
        send(rows(mix, 0, tok), rows(mix, slot1, tok), dev(dx=1)),
        send(rows(mix, 0, tok), rows(mix, slot2, tok), dev(dx=-1)),
    ]

    def transpose(src, dst, pair):
        r = pl.ds(pair * 2 * tok, 2 * tok)
        for b in range(width // 128):
            v = src[r, pl.ds(b * 128, 128)].T
            for q in range(4):
                dst[q % 2, pl.ds(q // 2 * 256 + b * 32, 32), r] = v[q * 32 : q * 32 + 32]

    weights = ((wg, wu, wd), (wg2, wu2, wd2))

    def proc_d(r0, n, h):
        wdr = weights[h][2]
        dh[pl.ds(r0, n), pl.ds(h * ff, ff)] = mm(cot[pl.ds(r0, n), :], wdr[...], NT)

    def proc_g(r0, n, h):
        wgr, wur, _ = weights[h]
        r = pl.ds(r0, n)
        for t in range(ff // 256):
            cs = pl.ds(t * 256, 256)
            oc = pl.ds(h * ff + t * 256, 256)
            gate = mm(mix[r, :], wgr[:, cs])
            value = mm(mix[r, :], wur[:, cs])
            dhid = dh[r, oc]
            sig = 1.0 / (1.0 + jnp.exp(-gate))
            act = gate * sig
            hid[r, oc] = (act * value).astype(BF16)
            dg[r, oc] = (dhid * value * sig * (1.0 + gate * (1.0 - sig))).astype(BF16)
            du[r, oc] = (dhid * act).astype(BF16)

    def back(r0, n):
        r = pl.ds(r0, n)
        for t in range(width // 512):
            cs = pl.ds(t * 512, 512)
            acc = None
            for h in range(2):
                wgr, wur, _ = weights[h]
                hs = pl.ds(h * ff, ff)
                a = mm(dg[r, hs], wgr[cs, :], NT) + mm(du[r, hs], wur[cs, :], NT)
                acc = a if acc is None else acc + a
            pb[r, cs] = acc.astype(BF16)

    def outp(r0, n):
        r = pl.ds(r0, n)
        for t in range(width // 512):
            cs = pl.ds(t * 512, 512)
            acc = mm(hid[r, pl.ds(0, ff)], wd[:, cs]) + mm(hid[r, pl.ds(ff, ff)], wd2[:, cs])
            po[r, cs] = acc.astype(BF16)

    def forward(copies, buf):
        copies[0].wait_recv()
        a = send(rows(buf, slot1, half), rows(buf, slot3, half), dev(dx=1))
        copies[1].wait_recv()
        b = send(rows(buf, slot2 + half, half), rows(buf, slot3 + half, half), dev(dx=-1))
        return [a, b]

    def share(i):
        cu, cd, other, n = c_w[i]
        cu.wait_recv()
        cd.wait_recv()
        return [
            send(rows(other, c * n, n), rows(other, c * n, n), dev(dc=1)),
            send(rows(other, (2 + c) * n, n), rows(other, (2 + c) * n, n), dev(dc=1)),
        ]

    proc_d(0, tok, 0)
    proc_g(0, tok, 0)
    c_share = share(0)
    f_cot = forward(c_cot, cot)
    proc_d(slot1, 2 * tok, 0)
    c_share += share(1)
    for cp in c_share:
        cp.wait_recv()
    transpose(cot, cot_t, 0)
    c_share2 = share(2)
    f_mix = forward(c_mix, mix)
    proc_d(0, 3 * tok, 1)
    for cp in c_share2:
        cp.wait_recv()
    proc_g(0, tok, 1)
    proc_g(slot1, 2 * tok, 0)
    proc_g(slot1, 2 * tok, 1)
    transpose(mix, mix_t, 0)
    back(0, 3 * tok)
    outp(0, 3 * tok)
    for cp in f_cot:
        cp.wait_recv()
    proc_d(slot3, tok, 0)
    proc_d(slot3, tok, 1)
    transpose(cot, cot_t, 1)
    for cp in f_mix:
        cp.wait_recv()

    def spread3(part, far):
        return [
            send(rows(part, slot3, half), far.at[0], dev(dx=-1)),
            send(rows(part, slot3 + half, half), far.at[1], dev(dx=1)),
        ]

    def spread1(part, near):
        return [
            send(rows(part, slot1 + half, half), near.at[0, pl.ds(half, half)], dev(dx=-1)),
            send(rows(part, slot2, half), near.at[1, pl.ds(0, half)], dev(dx=1)),
        ]

    def merge(part, far, copies, near):
        copies[0].wait_recv()
        r = pl.ds(slot1, half)
        part[r, :] = (part[r, :].astype(F32) + far[0].astype(F32)).astype(BF16)
        a = send(rows(part, slot1, half), near.at[0, pl.ds(0, half)], dev(dx=-1))
        copies[1].wait_recv()
        r = pl.ds(slot2 + half, half)
        part[r, :] = (part[r, :].astype(F32) + far[1].astype(F32)).astype(BF16)
        b = send(rows(part, slot2 + half, half), near.at[1, pl.ds(half, half)], dev(dx=1))
        return [a, b]

    def weight_grad(g, u, lhs, rhs):
        cp = None
        for cc in (1 - c, c):
            for h in range(2):
                yl2 = yl if h == 0 else 1 - yl
                v = mm(lhs[cc], rhs[:, pl.ds(h * ff + u * cols_u, cols_u)]) * grad_scale
                for yh2 in range(2):
                    gb[g, cc, u, yh2 * 2 + yl2] = v[yh2 * 256 : yh2 * 256 + 256].astype(BF16)
            if cp is None:
                cp = send(gb.at[g, cc, u], rc.at[g, u], dev(dc=1))
        return cp

    def add_core(g, u, cp):
        cp.wait_recv()
        for t in range(NY):
            gb[g, c, u, t] = (gb[g, c, u, t].astype(F32) + rc[g, u, t].astype(F32)).astype(BF16)

    yup, ydown, yfar = lax.rem(y + 1, NY), lax.rem(y + 3, NY), lax.rem(y + 2, NY)
    n_y = gb.shape[4]
    lo, hi = pl.ds(0, n_y // 2), pl.ds(n_y // 2, n_y // 2)

    def y_first(g, u):
        far = [
            send(gb.at[g, c, u, yfar, lo], ry2.at[g, u, 0], dev(dy=-1)),
            send(gb.at[g, c, u, yfar, hi], ry2.at[g, u, 1], dev(dy=1)),
        ]
        near = [
            send(gb.at[g, c, u, ydown, hi], ry1.at[g, u, 0, hi], dev(dy=-1)),
            send(gb.at[g, c, u, yup, lo], ry1.at[g, u, 1, lo], dev(dy=1)),
        ]
        return far, near

    def y_merge(g, u, cps):
        far, near = cps
        for i, (to, part, sign) in enumerate(((ydown, lo, -1), (yup, hi, 1))):
            far[i].wait_recv()
            v = gb[g, c, u, to, part].astype(F32) + ry2[g, u, i].astype(F32)
            gb[g, c, u, to, part] = v.astype(BF16)
            near.append(send(gb.at[g, c, u, to, part], ry1.at[g, u, i, part], dev(dy=sign)))
        return near

    def y_last(g, u, near):
        for cp in near:
            cp.wait_recv()
        v = gb[g, c, u, y].astype(F32) + ry1[g, u, 0].astype(F32) + ry1[g, u, 1].astype(F32)
        gz[g, u] = v.astype(BF16).reshape(NZ, 32, cols_u)
        return [
            send(gz.at[g, u, lax.rem(z + d, NZ)], rz.at[g, u, d - 1], dev(dz=d))
            for d in (4, 3, 5, 2, 6, 1, 7)
        ]

    def z_last(g, u, cps, out):
        for cp in cps:
            cp.wait_recv()
        v = gz[g, u, z].astype(F32)
        for d in range(NZ - 1):
            v = v + rz[g, u, d].astype(F32)
        out[:, pl.ds(u * cols_u, cols_u)] = v

    def stripe(d, r0, n):
        return pl.ds(pl.multiple_of(lax.rem(z + d + NZ, NZ) * 32 + r0, 16), n)

    def z_step(k, u, cps):
        new = []
        for way, sign in ((0, 1), (1, -1)):
            if k == 1:
                st, r = stripe(4, way * 16, 16), pl.ds(way * 16, 16)
                new.append(send(gb.at[2, c, u, :, st], zr.at[u, way, 0, :, r], dev(dz=sign)))
                continue
            cps[way].wait_recv()
            if k == 2:
                st, r = stripe(3 * sign, way * 16, 16), pl.ds(way * 16, 16)
            else:
                st, r = stripe((5 - k) * sign, 0, 32), pl.ds(0, 32)
            v = gb[2, c, u, :, st].astype(F32) + zr[u, way, k - 2, :, r].astype(F32)
            gb[2, c, u, :, st] = v.astype(BF16)
            st = stripe((5 - k) * sign, 0, 32)
            new.append(send(gb.at[2, c, u, :, st], zr.at[u, way, k - 1], dev(dz=sign)))
        return new

    def z_done(u, cps):
        for cp in cps:
            cp.wait_recv()
        st = stripe(0, 0, 32)
        v = gb[2, c, u, :, st].astype(F32) + zr[u, 0, 3].astype(F32) + zr[u, 1, 3].astype(F32)
        gy[u] = v.astype(BF16)
        return [
            send(gy.at[u, lax.rem(y + d, NY)], rzy.at[u, d - 1], dev(dy=d)) for d in range(1, NY)
        ]

    def zy_last(u, cps, out):
        for cp in cps:
            cp.wait_recv()
        v = gy[u, y].astype(F32)
        for d in range(NY - 1):
            v = v + rzy[u, d].astype(F32)
        out[:, pl.ds(u * cols_u, cols_u)] = v

    leaving = []

    def leave(src, dst):
        cp = pltpu.make_async_copy(src, dst, lsem.at[5 + len(leaving)])
        cp.start()
        leaving.append(cp)

    def total(part, near, copies, store):
        for cp in copies:
            cp.wait_recv()
        for j in range(4):
            r = pl.ds(j * lat, lat)
            v = part[r, :].astype(F32) + near[0, r, :].astype(F32) + near[1, r, :].astype(F32)
            store(j, v.astype(BF16))

    def store_dm(j, v):
        dm[j] = v

    def kernel_tile(e):
        cs = pl.ds(e * 128, 128)
        cols = [halo[0, :, cs]] + [f_ref[j, :, cs] for j in range(4)] + [halo[1, :, cs]]
        cols = [v.astype(F32) for v in cols]
        sums = [None] * 9
        for j in range(4):
            d = dm[j, :, cs].astype(F32)
            for a, v in enumerate((up(d), d, down(d))):
                for b in range(3):
                    p = v * cols[j + b]
                    i = 3 * a + b
                    sums[i] = p if sums[i] is None else sums[i] + p
        for i in range(9):
            kp[e, pl.ds(i, 1), :] = jnp.sum(sums[i], axis=0, keepdims=True) * grad_scale

    me = 2 * x + c

    def kernel_terms():
        kp[...] = jnp.zeros(kp.shape, F32)
        for e in range(NX * NC):
            kernel_tile(e)
        cps = []
        for i, (dx, dc) in enumerate(squad):
            to = 2 * lax.rem(x + dx, NX) + lax.rem(c + dc, NC)
            cps.append(send(kp.at[to], rk1.at[i], dev(dx=dx, dc=dc)))
        return cps

    def kernel_y(cps):
        for cp in cps:
            cp.wait_recv()
        v = kp[me]
        for i in range(len(squad)):
            v = v + rk1[i]
        rk2[y] = v
        return [send(rk2.at[y], rk2.at[y], dev(dy=d)) for d in range(1, NY)]

    def kernel_z(cps):
        for cp in cps:
            cp.wait_recv()
        rk3[z] = rk2[0] + rk2[1] + rk2[2] + rk2[3]
        return [send(rk3.at[z], rk3.at[z], dev(dz=d)) for d in range(1, NZ)]

    def kernel_all(cps):
        for cp in cps:
            cp.wait_recv()
        v = rk3[0]
        for i in range(1, NZ):
            v = v + rk3[i]
        kf[me] = v
        return [send(kf.at[me], kf.at[me], dev(dx=dx, dc=dc)) for dx, dc in squad]

    def kernel_last(cps):
        for cp in cps:
            cp.wait_recv()
        for e in range(NX * NC):
            for a in range(3):
                for b in range(3):
                    o_gk[a, pl.ds(b, 1), pl.ds(e * 128, 128)] = kf[e, pl.ds(3 * a + b, 1), :]

    def store_in(j, cs, v):
        tmp[j, :, cs] = v

    def store_out(j, v):
        tmp[j] = v

    c_b1 = spread1(pb, rb1)
    proc_g(slot3, tok, 0)
    proc_g(slot3, tok, 1)
    back(slot3, tok)
    c_b3 = spread3(pb, rb3)
    transpose(mix, mix_t, 1)
    g00 = weight_grad(0, 0, mix_t, dg)
    g20 = weight_grad(2, 0, cot_t, hid)
    g01 = weight_grad(0, 1, mix_t, dg)
    add_core(0, 0, g00)
    y00 = y_first(0, 0)
    g21 = weight_grad(2, 1, cot_t, hid)
    add_core(2, 0, g20)
    za = z_step(1, 0, None)
    g10 = weight_grad(1, 0, mix_t, du)
    add_core(0, 1, g01)
    y01 = y_first(0, 1)
    g11 = weight_grad(1, 1, mix_t, du)
    c_b1 += merge(pb, rb3, c_b3, rb1)
    add_core(2, 1, g21)
    zb = z_step(1, 1, None)
    y00 = y_merge(0, 0, y00)
    za = z_step(2, 0, za)
    outp(slot3, tok)
    add_core(1, 0, g10)
    y10 = y_first(1, 0)
    zb = z_step(2, 1, zb)
    add_core(1, 1, g11)
    y11 = y_first(1, 1)
    y01 = y_merge(0, 1, y01)
    za = z_step(3, 0, za)
    total(pb, rb1, c_b1, store_dm)
    c_dh = [send(dm.at[3], dhalo.at[0], lon_up), send(dm.at[0], dhalo.at[1], lon_down)]
    c_k = kernel_terms()
    c_o3 = spread3(po, ro3)
    c_o1 = spread1(po, ro1)
    y00 = y_last(0, 0, y00)
    c_k = kernel_y(c_k)
    zb = z_step(3, 1, zb)
    y10 = y_merge(1, 0, y10)
    za = z_step(4, 0, za)
    c_k = kernel_z(c_k)
    y11 = y_merge(1, 1, y11)
    y01 = y_last(0, 1, y01)
    c_k = kernel_all(c_k)
    zb = z_step(4, 1, zb)
    c_o1 += merge(po, ro3, c_o3, ro1)
    for cp in c_dh:
        cp.wait_recv()
    conv(dm, dhalo, True, store_in)
    o_in[...] = jnp.swapaxes(tmp[...], 0, 1)
    leave(o_in, h_in)
    za = z_done(0, za)
    y10 = y_last(1, 0, y10)
    y11 = y_last(1, 1, y11)
    zb = z_done(1, zb)
    z_last(0, 0, y00, o_gg)
    z_last(0, 1, y01, o_gg)
    leave(o_gg, h_gg)
    total(po, ro1, c_o1, store_out)
    o_out[...] = jnp.swapaxes(tmp[...], 0, 1)
    leave(o_out, h_out)
    kernel_last(c_k)
    leave(o_gk, h_gk)
    zy_last(0, za, o_gd)
    zy_last(1, zb, o_gd)
    leave(o_gd, h_gd)
    z_last(1, 0, y10, o_gu)
    z_last(1, 1, y11, o_gu)
    leave(o_gu, h_gu)
    for cp in started:
        cp.wait_send()
    for cp in leaving:
        cp.wait()


def place(*refs):
    for src, dst in zip(refs[:6], refs[6:]):
        dst[...] = src[...]


def shards(fields, conv_kernel, gate_weight, up_weight, down_weight, cotangent):
    _, lat, lon, width = fields.shape
    ff = gate_weight.shape[1]
    tok = lat * lon
    total_tokens = tok * lax.axis_size("shard") * lax.axis_size("lon")
    grad_scale = 1.0 / float(total_tokens) ** 0.5
    rows_d = width // 32
    vmem = lambda *shape, dtype=BF16: pltpu.VMEM(shape, dtype)
    call = pl.pallas_call(
        lambda *refs: kernel(grad_scale, *refs),
        name="swiglu_block",
        out_shape=[
            jax.ShapeDtypeStruct((lat, lon, width), BF16),
            jax.ShapeDtypeStruct((lat, lon, width), BF16),
            jax.ShapeDtypeStruct((rows_d, ff), F32),
            jax.ShapeDtypeStruct((rows_d, ff), F32),
            jax.ShapeDtypeStruct((rows_d, ff), F32),
            jax.ShapeDtypeStruct((3, 3, width), F32),
        ],
        in_specs=[pl.BlockSpec(memory_space=pltpu.VMEM if i == 1 else pl.ANY) for i in range(6)],
        out_specs=[pl.BlockSpec(memory_space=pl.ANY)] * 6,
        scratch_shapes=[
            vmem(lat, lon, width),
            vmem(lat, lon, width),
            vmem(rows_d, ff, dtype=F32),
            vmem(rows_d, ff, dtype=F32),
            vmem(rows_d, ff, dtype=F32),
            vmem(3, 3, width, dtype=F32),
            vmem(lon, lat, width),
            vmem(lat, lon, width),
            vmem(lat, lon, width),
            vmem(lon, lat, width),
            vmem(width, ff),
            vmem(width, ff),
            vmem(ff, width),
            vmem(2, lat, width),
            vmem(2, lat, width),
            vmem(width, ff),
            vmem(width, ff),
            vmem(ff, width),
            vmem(4 * tok, width),
            vmem(4 * tok, width),
            vmem(4 * tok, 2 * ff),
            vmem(4 * tok, 2 * ff),
            vmem(4 * tok, 2 * ff),
            vmem(4 * tok, width),
            vmem(4 * tok, width),
            vmem(2, tok // 2, width),
            vmem(2, tok, width),
            vmem(2, tok // 2, width),
            vmem(2, tok, width),
            vmem(4 * tok, 2 * ff, dtype=F32),
            vmem(2, width // 2, 4 * tok),
            vmem(2, width // 2, 4 * tok),
            vmem(3, 2, 2, NY, width // 4, ff // 2),
            vmem(3, 2, NY, width // 4, ff // 2),
            vmem(2, 2, 2, width // 8, ff // 2),
            vmem(2, 2, 2, width // 4, ff // 2),
            vmem(2, 2, NZ, 32, ff // 2),
            vmem(2, 2, NZ - 1, 32, ff // 2),
            vmem(2, 2, 4, NY, 32, ff // 2),
            vmem(2, NY, 32, ff // 2),
            vmem(2, NY - 1, 32, ff // 2),
            vmem(lon, lat, width),
            vmem(8, 16, width // 8, dtype=F32),
            vmem(7, 16, width // 8, dtype=F32),
            vmem(NY, 16, width // 8, dtype=F32),
            vmem(NZ, 16, width // 8, dtype=F32),
            vmem(8, 16, width // 8, dtype=F32),
            pltpu.SemaphoreType.DMA((N_SEM,)),
            pltpu.SemaphoreType.DMA((N_SEM,)),
            pltpu.SemaphoreType.DMA((11,)),
        ],
        compiler_params=pltpu.CompilerParams(
            collective_id=0, has_side_effects=True, vmem_limit_bytes=60 * 2**20
        ),
        cost_estimate=pl.CostEstimate(flops=14_500_000_000, bytes_accessed=6_000_000, transcendentals=800_000),
    )
    out, in_grad, gg, gu, gd, gk = call(
        fields[0], conv_kernel, gate_weight, up_weight, down_weight, cotangent[0]
    )

    results = (out, in_grad, gg, gu, gd, gk)
    out, in_grad, gg, gu, gd, gk = pl.pallas_call(
        place,
        name="place",
        out_shape=[jax.ShapeDtypeStruct(v.shape, v.dtype) for v in results],
        in_specs=[pl.BlockSpec(memory_space=pltpu.VMEM)] * 6,
        out_specs=[pl.BlockSpec(memory_space=pltpu.VMEM)] * 6,
    )(*results)
    return out[None], in_grad[None], gg, gu, gd.T, gk


def solution(mesh):
    placed = (
        P("shard", None, "lon", None),
        P(),
        P(None, "shard"),
        P(None, "shard"),
        P("shard", None),
        P("shard", None, "lon", None),
    )
    return jax.shard_map(
        shards,
        mesh=mesh,
        in_specs=placed,
        out_specs=(
            P("shard", None, "lon", None),
            P("shard", None, "lon", None),
            P("lon", "shard"),
            P("lon", "shard"),
            P("shard", "lon"),
            P(),
        ),
        check_vma=False,
    )
```
